128 devices in a mesh: sec: 2 (over core), elem: 64 (over x, y, z).
Axes of the slice: x: 4, y: 4, z: 4, core: 2. Of those that a mesh axis runs over, the one named last changes fastest.
Arguments:
- fields: float32 [2, 320, 65536], P('sec', None, 'elem'), may hold values from -6 to 6
- jacobian: float32 [2, 65536], P('sec', 'elem'), may hold values from 0.25 to 2.5
- face_links: int32 [2, 6, 65536], P('sec', None, 'elem'), may hold values from 0 to 1535, as said below
- volume_matrix: float32 [2, 320, 320], P('sec'), may hold values from -0.3125 to 0.3125
- face_matrices: float32 [2, 6, 320, 320], P('sec'), may hold values from -0.3125 to 0.3125
- patterns: float32 [4, 64, 64], replicated, may hold values from 0 to 0.03125
- donor_index: int32 [2, 32768], P('sec', 'elem'), may hold values from 0 to 1023
- pattern_index: int32 [2, 32768], P('sec', 'elem'), may hold values from 0 to 3
- receivers: int32 [2, 32768], P('sec', 'elem'), may hold values from -1 to 1023, as said below
Outputs:
- advanced: float32 [2, 320, 65536], P('sec', None, 'elem')
The draws below stay inside these ranges and needn't reach their ends.
Inputs may be any that keep to these rules, and one draw needn't show every extreme that they name: face_links[s, f, g] counts from the lowest rim element of the device holding element g; index 256 is that device's first own element. receivers holds on each device 8 slots for each device of the other section, source-major; -1 marks an empty slot, other entries on one device are distinct; in every draw some device gets 8 blocks from every device of the other section.
All inputs are finite; a program needn't handle non-finite values.
Results may differ from the reference program's by a relative error of at most 0.0001.
Values sent between devices are 32-bit elements; how exact they have to be, the bound alone decides.
No kernel may reach another device: no remote copies, remote signals or barrier semaphores. Data moves between devices by JAX's collectives and lax.ppermute only.
A program may use at most 64 MiB of HBM per device.

```python
import math
import jax
import jax.numpy as jnp
from jax import lax

VARS = 5
NODES = 64
E_DEV = 1024
HALO = 256
CAP = 8
NPAT = 4
COMPONENTS = 320
NE = 65536
SLOTS = 512
TOTAL_SLOTS = 32768
N_ELEM = 64


def draw_face_links(key, part):
    subkeys = jax.random.split(jax.random.fold_in(key, 7), 3)
    grid_shape = (2, 6, NE)
    position = jnp.arange(NE, dtype=jnp.int32) % E_DEV
    near_reach = min(16, HALO)
    short_reach = jax.random.randint(subkeys[0], grid_shape, 1, near_reach + 1, dtype=jnp.int32)
    medium = jax.random.randint(subkeys[1], grid_shape, 1, HALO // 2 + 1, dtype=jnp.int32)
    far_reach = jax.random.randint(subkeys[2], grid_shape, HALO // 2, HALO + 1, dtype=jnp.int32)
    distance = jnp.concatenate([short_reach[:, 0:2], medium[:, 2:4], far_reach[:, 4:6]], axis=1)
    direction = jnp.array([-1, 1, -1, 1, -1, 1], jnp.int32)[None, :, None]
    neighbours = position[None, None, :] + HALO + direction * distance
    face_ids = jnp.arange(6, dtype=jnp.int32)[None, :, None]
    neighbours = jnp.where((face_ids == 4) & (position == 0)[None, None, :], 0, neighbours)
    neighbours = jnp.where((face_ids == 5) & (position == E_DEV - 1)[None, None, :], E_DEV + 2 * HALO - 1, neighbours)
    return neighbours.astype(jnp.int32)


def draw_receivers(key, part):
    sections = []
    for section in range(2):
        subkeys = jax.random.split(jax.random.fold_in(key, 11 + section), 3)
        counts = jax.random.randint(subkeys[0], (N_ELEM, N_ELEM), CAP // 2, CAP + 1, dtype=jnp.int32)
        source = jnp.arange(N_ELEM, dtype=jnp.int32)[:, None]
        target = jnp.arange(N_ELEM, dtype=jnp.int32)[None, :]
        quarter = N_ELEM // 4
        reach = 3 * N_ELEM // 4
        if section == 1:
            banded = (target - source // quarter * quarter) % N_ELEM < reach
        else:
            banded = (source - target // quarter * quarter) % N_ELEM < reach
        busiest = jax.random.randint(subkeys[1], (), 0, N_ELEM, dtype=jnp.int32)
        counts = jnp.where(target == busiest, CAP, jnp.where(banded, counts, 0))
        orders = jax.vmap(lambda subkey: jax.random.permutation(subkey, E_DEV))(jax.random.split(subkeys[2], N_ELEM)).astype(jnp.int32)
        leading = orders[:, :1]
        orders = jnp.where(orders == E_DEV - 1, leading, orders)
        orders = orders.at[:, 0].set(E_DEV - 1)
        slot_number = jnp.arange(N_ELEM * CAP, dtype=jnp.int32)
        sender = slot_number // CAP
        within = slot_number % CAP
        limit = jnp.transpose(counts)[:, sender]
        values = jnp.where(within[None, :] < limit, orders[:, :N_ELEM * CAP], -1)
        sections.append(values.reshape(-1))
    return jnp.stack(sections).astype(jnp.int32)


def set_ends(values, key, smallest, top_value):
    shape = values.shape
    spot = [jax.random.randint(jax.random.fold_in(key, axis), (), 0, shape[axis]) for axis in range(len(shape))]
    values = values.at[tuple(spot)].set(smallest)
    longest = shape.index(max(shape))
    spot[longest] = (spot[longest] + 1) % shape[longest]
    return values.at[tuple(spot)].set(top_value)


def levels(key, extent, pieces, smallest, top_value):
    def one(dim, blocks):
        draws = jax.random.uniform(jax.random.fold_in(jax.random.fold_in(key, 6), dim), (blocks,), jnp.float32, smallest / len(pieces), top_value / len(pieces))
        return jnp.repeat(jnp.exp(draws), extent[dim] // blocks).reshape((-1,) + (1,) * (len(extent) - dim - 1))

    gain = one(*pieces[0])
    for cut in pieces[1:]:
        gain = gain * one(*cut)
    return gain


def noise(key, dims, spread, bound, cuts=(), kind=jnp.bfloat16):
    drawn = jax.random.normal(key, dims, jnp.float32) * spread
    if len(cuts) > 0:
        drawn = levels(key, dims, cuts, -0.22, 0.18) * drawn
    return jnp.clip(drawn, min=-bound, max=bound).astype(kind)


def setup_inputs(seed: int = 0) -> dict:
    seeds = jax.random.split(jax.random.key(seed), 10)
    return {
        "fields": noise(seeds[0], (2, COMPONENTS, NE), 1.0, 6.0, ((0, 2), (2, 64)), jnp.float32),
        "jacobian": jnp.clip(jnp.exp(math.log(2.5) - 2.3025851 * jax.random.uniform(seeds[1], (2, NE), jnp.float32) ** levels(seeds[1], (2, NE), ((0, 2), (1, 64)), -0.2, 0.2)), 0.25, 2.5),
        "face_links": draw_face_links(jax.random.fold_in(seeds[9], 71), 0),
        "volume_matrix": noise(seeds[3], (2, COMPONENTS, COMPONENTS), COMPONENTS ** -0.5, 0.3125, ((0, 2),), jnp.float32),
        "face_matrices": noise(seeds[4], (2, 6, COMPONENTS, COMPONENTS), COMPONENTS ** -0.5, 0.3125, ((0, 2),), jnp.float32),
        "patterns": jnp.clip(jax.random.uniform(seeds[5], (NPAT, NODES, NODES), jnp.float32, 0.0, 0.03125), 0.0, 0.03125),
        "donor_index": set_ends(jax.random.randint(seeds[6], (2, TOTAL_SLOTS), 0, E_DEV), jax.random.fold_in(seeds[6], 1), 0, E_DEV - 1).astype(jnp.int32),
        "pattern_index": set_ends(jax.random.randint(seeds[7], (2, TOTAL_SLOTS), 0, NPAT), jax.random.fold_in(seeds[7], 1), 0, NPAT - 1).astype(jnp.int32),
        "receivers": draw_receivers(jax.random.fold_in(seeds[9], 71), 0),
    }


time_step = 0.25


def section_rate(values, inverse_volume, neighbours, volume_block, face_blocks):
    padded = jnp.pad(values, ((0, 0), (HALO, HALO)))
    element = jnp.arange(NE, dtype=jnp.int32)
    anchor = (element // E_DEV) * E_DEV
    summed = jnp.dot(volume_block, values, precision=lax.Precision.HIGHEST, preferred_element_type=jnp.float32)
    for direction in range(6):
        column = (anchor + neighbours[direction]).astype(jnp.int32)
        summed = summed + jnp.dot(face_blocks[direction], jnp.take(padded, column, axis=1), precision=lax.Precision.HIGHEST, preferred_element_type=jnp.float32)
    return inverse_volume[None, :] * summed


def interpolate(values, donors, choose, patterns):
    columns = jnp.take(values, donors, axis=1).reshape(VARS, NODES, -1)
    result = jnp.zeros_like(columns)
    for which_one in range(NPAT):
        mapped = jnp.einsum("mn,vnc->vmc", patterns[which_one], columns, precision=lax.Precision.HIGHEST)
        result = jnp.where(choose[None, None, :] == which_one, mapped, result)
    return result.reshape(VARS * NODES, -1)


def fringe(fields, donor_index, pattern_index, receivers, patterns):
    slot_owner = jnp.arange(TOTAL_SLOTS, dtype=jnp.int32) // SLOTS
    blocks = []
    for section in range(2):
        donors = (slot_owner * E_DEV + donor_index[section]).astype(jnp.int32)
        blocks.append(interpolate(fields[section], donors, pattern_index[section], patterns))
    updated = []
    for section in range(2):
        source = blocks[1 - section].reshape(VARS * NODES, N_ELEM, N_ELEM, CAP)
        source = jnp.transpose(source, (0, 2, 1, 3)).reshape(VARS * NODES, TOTAL_SLOTS)
        target = receivers[section]
        place = jnp.where(target >= 0, slot_owner * E_DEV + target, NE).astype(jnp.int32)
        updated.append(fields[section].at[:, place].set(source, mode="drop"))
    return jnp.stack(updated)


def rate(values, jacobian, face_links, volume_matrix, face_matrices):
    return jnp.stack([section_rate(values[section], jacobian[section], face_links[section], volume_matrix[section], face_matrices[section]) for section in range(2)])


def reference(fields, jacobian, face_links, volume_matrix, face_matrices, patterns, donor_index, pattern_index, receivers):
    first_segment = fringe(fields, donor_index, pattern_index, receivers, patterns)
    middle = first_segment + time_step * rate(first_segment, jacobian, face_links, volume_matrix, face_matrices)
    second = fringe(middle, donor_index, pattern_index, receivers, patterns)
    return 0.5 * first_segment + 0.5 * (second + time_step * rate(second, jacobian, face_links, volume_matrix, face_matrices))
```

```python
import jax
import jax.numpy as jnp
from jax import lax
from jax.experimental import pallas as pl
from jax.experimental.pallas import tpu as pltpu
from jax.sharding import PartitionSpec as P

NPAT = 4
HALO = 256
ELEMS = 1024
SLOTS = 512
LANES = 128
STATE_ROWS = ELEMS * 3
PAD_ROWS = 24
MESSAGE_ROWS = SLOTS * 3
LOCAL_PAIR = (ELEMS + 8) * 5
HALO_PAIR = (2 * HALO + 8) * 5
PRODUCT_TILES = 18
VMEM_LIMIT = 56 * 1024 * 1024

VMEM = pl.BlockSpec(memory_space=pltpu.VMEM)
SMEM = pl.BlockSpec(memory_space=pltpu.SMEM)


def row(ref, start):
    return ref[pl.ds(start, 3, stride=8), :]


def put_row(ref, start, value):
    ref[pl.ds(start, 3, stride=8), :] = value


def tiles_of(value, count):
    return value.reshape(count // 8, 3, 8, LANES)


def split(value):
    high = value.astype(jnp.bfloat16).astype(jnp.float32)
    return high, value - high


def fill_operand(x_ref, columns):
    h0, l0 = split(columns[0])
    h1, l1 = split(columns[1])
    h2, l2 = split(columns[2])
    both = h2 + pltpu.roll(l2, 64, 1)
    for k, part in enumerate((h0, h1, l0, l1, h0, h1, both, h2)):
        x_ref[:, k * LANES : (k + 1) * LANES] = part.astype(jnp.bfloat16)


def multiply(x_ref, w_ref, count, pair_rows, table, own, pairs_only):
    groups = count // 8
    for n in range((15 if pairs_only else PRODUCT_TILES) // 2 + (1 if pairs_only else 0)):
        product = jnp.dot(
            x_ref[...], w_ref[:, n * 256 : (n + 1) * 256], preferred_element_type=jnp.float32
        )
        for half in range(2):
            tile = 2 * n + half
            block = product[:, half * LANES : (half + 1) * LANES].reshape(groups, 8, LANES)
            if tile < 15:
                first = (tile // 5) * pair_rows
                for r in range(groups):
                    table[pl.ds(first + r * 40 + (tile % 5) * 8, 8), :] = block[r]
            elif not pairs_only:
                for r in range(groups):
                    own[pl.ds(r * 24 + (tile - 15) * 8, 8), :] = block[r]


def gather_group(table, where_ref, block, even_ref, odd_ref):
    for s in range(8):
        g = block * 8 + s
        even = row(table, where_ref[g])
        odd = row(table, where_ref[ELEMS + g])
        for face in range(2, 6, 2):
            even = even + row(table, where_ref[face * ELEMS + g])
            odd = odd + row(table, where_ref[(face + 1) * ELEMS + g])
        put_row(even_ref, block * 24 + s, even)
        put_row(odd_ref, block * 24 + s, odd)


def join(even_ref, odd_ref):
    even = tiles_of(even_ref[...], ELEMS)
    odd = tiles_of(odd_ref[...], ELEMS)
    last = (even[:, 2].reshape(ELEMS, LANES), odd[:, 0].reshape(ELEMS, LANES))
    lane = lax.broadcasted_iota(jnp.int32, (ELEMS, LANES), 1)
    last = jnp.where(lane < 64, last[0] + pltpu.roll(last[1], 64, 1), 0.0)
    return (
        (even[:, 0] + odd[:, 1]).reshape(ELEMS, LANES),
        (even[:, 1] + odd[:, 2]).reshape(ELEMS, LANES),
        last,
    )


def columns_of(ref):
    value = tiles_of(ref[0:STATE_ROWS, :], ELEMS)
    return [value[:, c].reshape(ELEMS, LANES) for c in range(3)]


def put_columns(ref, columns):
    stacked = jnp.stack([c.reshape(ELEMS // 8, 8, LANES) for c in columns], axis=1)
    ref[0:STATE_ROWS, :] = stacked.reshape(STATE_ROWS, LANES)


def send_blocks(state_ref, donors_ref, choose_ref, patterns_ref, out_ref, picked, operand):
    def body(block, carry):
        for s in range(8):
            put_row(picked, block * 24 + s, row(state_ref, donors_ref[block * 8 + s]))
        return carry

    lax.fori_loop(0, SLOTS // 8, body, 0)
    high, low = split(picked[...])
    for k, part in enumerate((high, low, high)):
        operand[:, k * LANES : (k + 1) * LANES] = part.astype(jnp.bfloat16)
    mapped = jnp.dot(operand[...], patterns_ref[...], preferred_element_type=jnp.float32)
    choose = choose_ref[...]
    result = mapped[:, :LANES]
    for which in range(1, NPAT):
        result = jnp.where(choose == which, mapped[:, which * LANES : (which + 1) * LANES], result)
    out_ref[...] = result


def start_kernel(fields_ref, donors_ref, choose_ref, patterns_ref, state_ref, out_ref, picked, operand):
    zero = jnp.zeros((64, LANES), jnp.float32)
    state_ref[STATE_ROWS:, :] = jnp.zeros((PAD_ROWS, LANES), jnp.float32)
    for block in range(ELEMS // LANES):
        lanes = slice(block * LANES, (block + 1) * LANES)
        for c in range(3):
            if c < 2:
                piece = fields_ref[c * LANES : (c + 1) * LANES, lanes]
            else:
                piece = jnp.concatenate([fields_ref[256:320, lanes], zero], axis=0)
            turned = piece.T
            for r in range(16):
                state_ref[pl.ds((block * 16 + r) * 24 + c * 8, 8), :] = turned[r * 8 : r * 8 + 8]
    send_blocks(state_ref, donors_ref, choose_ref, patterns_ref, out_ref, picked, operand)


def place_kernel(state_ref, arrived_ref, targets_ref, new_ref, low_ref, high_ref):
    new_ref[...] = state_ref[...]

    def body(block, carry):
        for s in range(8):
            put_row(new_ref, targets_ref[block * 8 + s], row(arrived_ref, block * 24 + s))
        return carry

    lax.fori_loop(0, SLOTS // 8, body, 0)
    for first, out in ((0, low_ref), (ELEMS - HALO, high_ref)):
        value = new_ref[first * 3 : (first + HALO) * 3, :].reshape(HALO // 8, 3, 8, LANES)
        out[0:256, :] = value[:, 0].reshape(HALO, LANES)
        out[256:512, :] = value[:, 1].reshape(HALO, LANES)
        last = value[:, 2].reshape(HALO, LANES)
        out[512:640, :] = last[0:128] + pltpu.roll(last[128:256], 64, 1)


def local_kernel(state_ref, matrix_ref, where_ref, sum_ref, x, table, even, odd):
    fill_operand(x, columns_of(state_ref))
    for pair in range(3):
        table[pl.ds(pair * LOCAL_PAIR + ELEMS * 5, 40), :] = jnp.zeros((40, LANES), jnp.float32)
    multiply(x, matrix_ref, ELEMS, LOCAL_PAIR, table, sum_ref, False)

    def body(block, carry):
        gather_group(table, where_ref, block, even, odd)
        return carry

    lax.fori_loop(0, ELEMS // 8, body, 0)
    put_columns(sum_ref, [a + b for a, b in zip(columns_of(sum_ref), join(even, odd))])


def halo_sums(low_ref, high_ref, matrix_ref, where_ref, active_ref, x, table, even, odd):
    lane = lax.broadcasted_iota(jnp.int32, (128, LANES), 1)
    columns = []
    for c in range(2):
        rows = slice(c * 256, (c + 1) * 256)
        columns.append(jnp.concatenate([low_ref[rows, :], high_ref[rows, :]], axis=0))
    last = []
    for ref in (low_ref, high_ref):
        both = ref[512:640, :]
        last.append(jnp.where(lane < 64, both, 0.0))
        last.append(jnp.where(lane < 64, pltpu.roll(both, 64, 1), 0.0))
    columns.append(jnp.concatenate(last, axis=0))
    fill_operand(x, columns)
    for pair in range(3):
        table[pl.ds(pair * HALO_PAIR + 2 * HALO * 5, 40), :] = jnp.zeros((40, LANES), jnp.float32)
    multiply(x, matrix_ref, 2 * HALO, HALO_PAIR, table, None, True)
    even[...] = jnp.zeros_like(even)
    odd[...] = jnp.zeros_like(odd)

    def body(block, carry):
        @pl.when(active_ref[block] > 0)
        def _():
            gather_group(table, where_ref, block, even, odd)

        return carry

    lax.fori_loop(0, ELEMS // 8, body, 0)
    return join(even, odd)


def middle_kernel(
    state_ref, sum_ref, low_ref, high_ref, matrix_ref, where_ref, active_ref, factor_ref,
    donors_ref, choose_ref, patterns_ref,
    new_ref, out_ref,
    x, table, even, odd, picked, operand,
):
    more = halo_sums(low_ref, high_ref, matrix_ref, where_ref, active_ref, x, table, even, odd)
    factor = factor_ref[...]
    put_columns(
        new_ref,
        [w + factor * (a + b) for w, a, b in zip(columns_of(state_ref), columns_of(sum_ref), more)],
    )
    new_ref[STATE_ROWS:, :] = jnp.zeros((PAD_ROWS, LANES), jnp.float32)
    send_blocks(new_ref, donors_ref, choose_ref, patterns_ref, out_ref, picked, operand)


def last_kernel(
    first_ref, state_ref, sum_ref, low_ref, high_ref, matrix_ref, where_ref, active_ref, factor_ref,
    out_ref,
    x, table, even, odd,
):
    more = halo_sums(low_ref, high_ref, matrix_ref, where_ref, active_ref, x, table, even, odd)
    factor = factor_ref[...]
    for c, (f, w, a, b) in enumerate(
        zip(columns_of(first_ref), columns_of(state_ref), columns_of(sum_ref), more)
    ):
        result = 0.5 * f + 0.5 * (w + factor * (a + b))
        turned = result.T
        if c < 2:
            out_ref[c * LANES : (c + 1) * LANES, :] = turned
        else:
            out_ref[256:320, :] = turned[0:64]


def params():
    return pltpu.CompilerParams(vmem_limit_bytes=VMEM_LIMIT)


def shape(rows, columns, dtype=jnp.float32):
    return jax.ShapeDtypeStruct((rows, columns), dtype)


def estimate(flops, size):
    return pl.CostEstimate(flops=flops, bytes_accessed=size, transcendentals=0)


STATE = shape(STATE_ROWS + PAD_ROWS, LANES)
MESSAGE = shape(MESSAGE_ROWS, LANES)
SEND_SCRATCH = [
    pltpu.VMEM((MESSAGE_ROWS, LANES), jnp.float32),
    pltpu.VMEM((MESSAGE_ROWS, 3 * LANES), jnp.bfloat16),
]


def sum_scratch(count, pair_rows):
    return [
        pltpu.VMEM((count, 1024), jnp.bfloat16),
        pltpu.VMEM((3 * pair_rows, LANES), jnp.float32),
        pltpu.VMEM((STATE_ROWS, LANES), jnp.float32),
        pltpu.VMEM((STATE_ROWS, LANES), jnp.float32),
    ]


def start(fields, donors, choose, patterns):
    return pl.pallas_call(
        start_kernel,
        out_shape=(STATE, MESSAGE),
        in_specs=[VMEM, SMEM, VMEM, VMEM],
        out_specs=(VMEM, VMEM),
        scratch_shapes=SEND_SCRATCH,
        compiler_params=params(),
        name="start",
    )(fields, donors, choose, patterns)


def place(state, arrived, targets):
    return pl.pallas_call(
        place_kernel,
        out_shape=(STATE, shape(640, LANES), shape(640, LANES)),
        in_specs=[VMEM, VMEM, SMEM],
        out_specs=(VMEM, VMEM, VMEM),
        compiler_params=params(),
        name="place",
    )(state, arrived, targets)


def local_sum(state, matrix, where):
    return pl.pallas_call(
        local_kernel,
        out_shape=shape(STATE_ROWS, LANES),
        in_specs=[VMEM, VMEM, SMEM],
        out_specs=VMEM,
        scratch_shapes=sum_scratch(ELEMS, LOCAL_PAIR),
        compiler_params=params(),
        cost_estimate=estimate(2 * 1024 * 1024 * 2304, 8 * 1024 * 1024),
        name="local_sum",
    )(state, matrix, where)


def middle_step(state, sums, low, high, matrix, where, active, factor, donors, choose, patterns):
    return pl.pallas_call(
        middle_kernel,
        out_shape=(STATE, MESSAGE),
        in_specs=[VMEM, VMEM, VMEM, VMEM, VMEM, SMEM, SMEM, VMEM, SMEM, VMEM, VMEM],
        out_specs=(VMEM, VMEM),
        scratch_shapes=sum_scratch(2 * HALO, HALO_PAIR) + SEND_SCRATCH,
        compiler_params=params(),
        name="middle_step",
    )(state, sums, low, high, matrix, where, active, factor, donors, choose, patterns)


def last_step(first, state, sums, low, high, matrix, where, active, factor):
    return pl.pallas_call(
        last_kernel,
        out_shape=shape(320, ELEMS),
        in_specs=[VMEM, VMEM, VMEM, VMEM, VMEM, VMEM, SMEM, SMEM, VMEM],
        out_specs=VMEM,
        scratch_shapes=sum_scratch(2 * HALO, HALO_PAIR),
        compiler_params=params(),
        name="last_step",
    )(first, state, sums, low, high, matrix, where, active, factor)


def halves(value):
    high = lax.reduce_precision(value, 8, 7)
    return high, value - high


def operator_matrix(volume, faces):
    own = volume.T
    face = [faces[f].T for f in range(6)]
    pieces = []
    for pair in range(3):
        even, odd = face[2 * pair], face[2 * pair + 1]
        pieces += [even, odd[:, 256:], odd[:, :256]]
    pieces += [own, jnp.zeros((320, 64), jnp.float32)]
    high, low = halves(jnp.concatenate(pieces, axis=1))
    rows = [high[:256], high[:256], low[:256], high[256:], high[256:], low[256:], jnp.zeros_like(high[:64])]
    return jnp.concatenate(rows, axis=0).astype(jnp.bfloat16)


def pattern_matrix(patterns):
    zero = jnp.zeros((64, 64), jnp.float32)
    blocks = []
    for which in range(NPAT):
        turned = patterns[which].T
        blocks.append(jnp.concatenate([
            jnp.concatenate([turned, zero], axis=1), jnp.concatenate([zero, turned], axis=1)
        ], axis=0))
    high, low = halves(jnp.concatenate(blocks, axis=1))
    return jnp.concatenate([high, high, low], axis=0).astype(jnp.bfloat16)


def state_row(element):
    return (element // 8) * 24 + element % 8


def product_rows(element, pair_rows):
    face = jnp.arange(6, dtype=jnp.int32)[:, None]
    spot = (face // 2) * pair_rows + (face % 2) * 16 + (element // 8) * 40 + element % 8
    return spot.reshape(-1)


def exchange(message):
    crossed = lax.ppermute(message, "sec", [(0, 1), (1, 0)])
    blocks = crossed.reshape(64, MESSAGE_ROWS // 64, LANES)
    return lax.all_to_all(blocks, "elem", 0, 0, tiled=True).reshape(MESSAGE_ROWS, LANES)


def rims(low, high):
    count = lax.axis_size("elem")
    up = [(i, i + 1) for i in range(count - 1)]
    down = [(i + 1, i) for i in range(count - 1)]
    return lax.ppermute(high, "elem", up), lax.ppermute(low, "elem", down)


def local(
    fields,
    jacobian,
    face_links,
    volume_matrix,
    face_matrices,
    patterns,
    donor_index,
    pattern_index,
    receivers,
):
    links = face_links[0]
    donors = state_row(donor_index[0])
    chosen = jnp.broadcast_to(
        pattern_index[0].reshape(SLOTS // 8, 1, 8, 1), (SLOTS // 8, 3, 8, LANES)
    ).reshape(MESSAGE_ROWS, LANES)
    pattern_blocks = pattern_matrix(patterns)
    targets = jnp.where(receivers[0] >= 0, state_row(receivers[0]), STATE_ROWS)

    state, message = start(fields[0], donors, chosen, pattern_blocks)

    own = (links >= HALO) & (links < HALO + ELEMS)
    local_rows = product_rows(jnp.where(own, links - HALO, ELEMS), LOCAL_PAIR)
    rim = jnp.where(links < HALO, links, links - ELEMS)
    halo_rows = product_rows(jnp.where(own, 2 * HALO, rim), HALO_PAIR)
    active = jnp.any((~own).reshape(6, ELEMS // 8, 8), axis=(0, 2)).astype(jnp.int32)
    factor = jnp.broadcast_to((0.25 * jacobian[0])[:, None], (ELEMS, LANES))
    matrix = operator_matrix(volume_matrix[0], face_matrices[0])

    arrived = exchange(message)
    first, low, high = place(state, arrived, targets)
    from_below, from_above = rims(low, high)
    sums = local_sum(first, matrix, local_rows)
    middle, message = middle_step(
        first, sums, from_below, from_above, matrix, halo_rows, active, factor,
        donors, chosen, pattern_blocks,
    )
    arrived = exchange(message)
    second, low, high = place(middle, arrived, targets)
    from_below, from_above = rims(low, high)
    sums = local_sum(second, matrix, local_rows)
    advanced = last_step(
        first, second, sums, from_below, from_above, matrix, halo_rows, active, factor
    )
    return advanced[None]


def solution(mesh):
    return jax.shard_map(
        local,
        mesh=mesh,
        in_specs=(
            P("sec", None, "elem"),
            P("sec", "elem"),
            P("sec", None, "elem"),
            P("sec", None, None),
            P("sec", None, None, None),
            P(),
            P("sec", "elem"),
            P("sec", "elem"),
            P("sec", "elem"),
        ),
        out_specs=P("sec", None, "elem"),
        check_vma=False,
    )
```

```python
import jax
import jax.numpy as jnp
from jax import lax
from jax.experimental import pallas as pl
from jax.experimental.pallas import tpu as pltpu
from jax.sharding import PartitionSpec as P

NPAT = 4
HALO = 256
ELEMS = 1024
SLOTS = 512
LANES = 128
STATE_ROWS = ELEMS * 3
PAD_ROWS = 24
MESSAGE_ROWS = SLOTS * 3
LOCAL_PAIR = ELEMS + 8
HALO_PAIR = 2 * HALO + 8
PRODUCT_TILES = 18
VMEM_LIMIT = 36 * 1024 * 1024

VMEM = pl.BlockSpec(memory_space=pltpu.VMEM)
SMEM = pl.BlockSpec(memory_space=pltpu.SMEM)
ANY = pl.BlockSpec(memory_space=pl.ANY)


def row(ref, start):
    return ref[pl.ds(start, 3, stride=8), :]


def put_row(ref, start, value):
    ref[pl.ds(start, 3, stride=8), :] = value


def tiles_of(value, count):
    return value.reshape(count // 8, 3, 8, LANES)


def split(value):
    high = value.astype(jnp.bfloat16).astype(jnp.float32)
    return high, value - high


def fill_operand(x_ref, columns):
    h0, l0 = split(columns[0])
    h1, l1 = split(columns[1])
    h2, l2 = split(columns[2])
    both = h2 + pltpu.roll(l2, 64, 1)
    for k, part in enumerate((h0, h1, l0, l1, h0, h1, both, h2)):
        x_ref[:, k * LANES : (k + 1) * LANES] = part.astype(jnp.bfloat16)


def multiply(x_ref, w_ref, count, pair_rows, table, own):
    groups = count // 8
    for n in range(9 if own is not None else 8):
        product = jnp.dot(
            x_ref[...], w_ref[:, n * 256 : (n + 1) * 256], preferred_element_type=jnp.float32
        )
        for half in range(2):
            tile = 2 * n + half
            block = product[:, half * LANES : (half + 1) * LANES].reshape(groups, 8, LANES)
            if tile < 15:
                first = (tile // 5) * pair_rows
                for r in range(groups):
                    table[pl.ds((first + r * 8) * 8 + tile % 5, 8, stride=8), :] = block[r]
            elif own is not None:
                for r in range(groups):
                    own[pl.ds(r * 24 + (tile - 15) * 8, 8), :] = block[r]
    for pair in range(3):
        table[pl.ds((pair * pair_rows + count) * 8, 8), :] = jnp.zeros((8, LANES), jnp.float32)


def tile_at(table, where_ref, position):
    return table[pl.ds(pl.multiple_of(where_ref[position], 8), 8), :]


def gather_group(table, where_ref, block, out_ref):
    sub = lax.broadcasted_iota(jnp.int32, (8, LANES), 0)
    lane = lax.broadcasted_iota(jnp.int32, (8, LANES), 1)
    from_even = (sub < 2) | ((sub == 2) & (lane < 64))
    for s in range(8):
        g = block * 8 + s
        even = tile_at(table, where_ref, g)
        odd = tile_at(table, where_ref, ELEMS + g)
        for face in range(2, 6, 2):
            even = even + tile_at(table, where_ref, face * ELEMS + g)
            odd = odd + tile_at(table, where_ref, (face + 1) * ELEMS + g)
        out_ref[pl.ds(pl.multiple_of(g * 8, 8), 8), :] = jnp.where(from_even, even, odd)


def join(ref):
    part = [ref[pl.ds(c, ELEMS, stride=8), :] for c in range(5)]
    lane = lax.broadcasted_iota(jnp.int32, (ELEMS, LANES), 1)
    last = jnp.where(lane < 64, part[2] + pltpu.roll(part[2], 64, 1), 0.0)
    return part[0] + part[3], part[1] + part[4], last


def columns_of(ref):
    value = tiles_of(ref[0:STATE_ROWS, :], ELEMS)
    return [value[:, c].reshape(ELEMS, LANES) for c in range(3)]


def put_columns(ref, columns):
    stacked = jnp.stack([c.reshape(ELEMS // 8, 8, LANES) for c in columns], axis=1)
    ref[0:STATE_ROWS, :] = stacked.reshape(STATE_ROWS, LANES)


def send_blocks(state_ref, donors_ref, choose_ref, patterns_ref, out_ref, picked, operand):
    def body(block, carry):
        for s in range(8):
            put_row(picked, block * 24 + s, row(state_ref, donors_ref[block * 8 + s]))
        return carry

    lax.fori_loop(0, SLOTS // 8, body, 0)
    high, low = split(picked[0:MESSAGE_ROWS])
    for k, part in enumerate((high, low, high)):
        operand[:, k * LANES : (k + 1) * LANES] = part.astype(jnp.bfloat16)
    mapped = jnp.dot(operand[...], patterns_ref[...], preferred_element_type=jnp.float32)
    choose = choose_ref[...].reshape(SLOTS // 8, 1, 8, LANES)
    result = tiles_of(mapped[:, :LANES], SLOTS)
    for which in range(1, NPAT):
        other = tiles_of(mapped[:, which * LANES : (which + 1) * LANES], SLOTS)
        result = jnp.where(choose == which, other, result)
    out_ref[...] = result.reshape(MESSAGE_ROWS, LANES)


def start_kernel(fields_ref, donors_ref, choose_ref, patterns_ref, out_ref, both, chosen):
    high, low = split(fields_ref[...])
    both[0:320, :] = high.astype(jnp.bfloat16)
    both[320:640, :] = low.astype(jnp.bfloat16)
    element = lax.broadcasted_iota(jnp.int32, (ELEMS, SLOTS), 0)
    chosen[...] = (element == donors_ref[...]).astype(jnp.float32).astype(jnp.bfloat16)
    picked = jnp.dot(both[...], chosen[...], preferred_element_type=jnp.float32)
    high = picked[0:320].astype(jnp.bfloat16)
    low = picked[320:640].astype(jnp.bfloat16)
    patterns_high, patterns_low = split(patterns_ref[...].reshape(NPAT * 64, 64))
    weights = jnp.concatenate([patterns_high, patterns_high, patterns_low], axis=1).astype(jnp.bfloat16)
    which = choose_ref[...]
    results = []
    for v in range(5):
        rows = slice(v * 64, (v + 1) * 64)
        operand = jnp.concatenate([high[rows], low[rows], high[rows]], axis=0)
        mapped = jnp.dot(weights, operand, preferred_element_type=jnp.float32)
        result = mapped[0:64]
        for p in range(1, NPAT):
            result = jnp.where(which == p, mapped[p * 64 : (p + 1) * 64], result)
        results.append(result)
    results.append(jnp.zeros((64, SLOTS), jnp.float32))
    for c in range(3):
        tall = jnp.concatenate([results[2 * c], results[2 * c + 1]], axis=0)
        for block in range(SLOTS // LANES):
            turned = tall[:, block * LANES : (block + 1) * LANES].T
            for r in range(16):
                out_ref[pl.ds((block * 16 + r) * 24 + c * 8, 8), :] = turned[r * 8 : r * 8 + 8]


def turn(piece):
    missing = LANES - piece.shape[0], LANES - piece.shape[1]
    if missing[1]:
        piece = jnp.concatenate([piece, jnp.zeros((piece.shape[0], missing[1]), jnp.float32)], axis=1)
    if missing[0]:
        piece = jnp.concatenate([piece, jnp.zeros((missing[0], LANES), jnp.float32)], axis=0)
    return piece.T


def put_words(out_ref, first, value):
    for k in range(value.shape[1] // LANES):
        out_ref[first + k : first + k + 1, :] = value[:, k * LANES : (k + 1) * LANES]


def prepare_kernel(
    fields_ref, jacobian_ref, links_ref, volume_ref, faces_ref, patterns_ref, donors_ref,
    choose_ref, targets_ref, after_ref,
    state_ref, factor_ref, matrix_ref, patterns_out, chosen_ref,
    local_ref, rim_ref, active_ref, slots_ref,
):
    del after_ref
    state_ref[STATE_ROWS:, :] = jnp.zeros((PAD_ROWS, LANES), jnp.float32)
    for block in range(ELEMS // LANES):
        lanes = slice(block * LANES, (block + 1) * LANES)
        for c in range(3):
            turned = turn(fields_ref[c * LANES : min((c + 1) * LANES, 320), lanes])
            for r in range(16):
                state_ref[pl.ds((block * 16 + r) * 24 + c * 8, 8), :] = turned[r * 8 : r * 8 + 8]
        scale = jnp.broadcast_to(0.25 * jacobian_ref[:, lanes], (LANES, LANES))
        factor_ref[lanes, :] = scale.T
    for block in range(SLOTS // LANES):
        lanes = slice(block * LANES, (block + 1) * LANES)
        which = jnp.broadcast_to(choose_ref[:, lanes].astype(jnp.float32), (LANES, LANES))
        chosen_ref[lanes, :] = which.T.astype(jnp.int32)
    for tile in range(PRODUCT_TILES):
        pair, kind = tile // 5, tile % 5
        columns = []
        for c in range(3):
            lanes = slice(c * LANES, min((c + 1) * LANES, 320))
            if tile >= 15:
                rows = slice((tile - 15) * LANES, min((tile - 14) * LANES, 320))
                piece = volume_ref[rows, lanes]
            elif kind == 2:
                piece = jnp.concatenate(
                    [faces_ref[2 * pair, 256:320, lanes], faces_ref[2 * pair + 1, 256:320, lanes]], axis=0
                )
            elif kind < 2:
                piece = faces_ref[2 * pair, kind * LANES : (kind + 1) * LANES, lanes]
            else:
                piece = faces_ref[2 * pair + 1, (kind - 3) * LANES : (kind - 2) * LANES, lanes]
            columns.append(turn(piece))
        h0, l0 = split(columns[0])
        h1, l1 = split(columns[1])
        h2, l2 = split(columns[2])
        twice = jnp.concatenate([h2[0:64], h2[0:64]], axis=0)
        at = slice(tile * LANES, (tile + 1) * LANES)
        for k, part in enumerate((h0, h1, h0, h1, l0, l1, twice, l2)):
            matrix_ref[k * LANES : (k + 1) * LANES, at] = part.astype(jnp.bfloat16)
    zero = jnp.zeros((64, 64), jnp.float32)
    for which in range(NPAT):
        one = patterns_ref[which]
        block = jnp.concatenate(
            [jnp.concatenate([one, zero], axis=1), jnp.concatenate([zero, one], axis=1)], axis=0
        )
        high, low = split(block.T)
        at = slice(which * LANES, (which + 1) * LANES)
        for k, part in enumerate((high, high, low)):
            patterns_out[k * LANES : (k + 1) * LANES, at] = part.astype(jnp.bfloat16)
    any_rim = jnp.zeros((1, ELEMS), jnp.int32)
    for face in range(6):
        links = links_ref[face : face + 1, :]
        own = (links >= HALO) & (links < HALO + ELEMS)
        pair = face // 2
        put_words(local_ref, face * 8, (jnp.where(own, links - HALO, ELEMS) + pair * LOCAL_PAIR) * 8)
        rim = jnp.where(links < HALO, links, links - ELEMS)
        put_words(rim_ref, face * 8, (jnp.where(own, 2 * HALO, rim) + pair * HALO_PAIR) * 8)
        any_rim = jnp.where(own, any_rim, 1)
    group = lax.broadcasted_iota(jnp.int32, (ELEMS, LANES), 0) // 8
    member = (group == lax.broadcasted_iota(jnp.int32, (ELEMS, LANES), 1)).astype(jnp.float32)
    spread = jnp.broadcast_to(any_rim.astype(jnp.float32), (8, ELEMS)).astype(jnp.bfloat16)
    active_ref[...] = jnp.dot(
        spread, member.astype(jnp.bfloat16), preferred_element_type=jnp.float32
    ).astype(jnp.int32)
    donors = donors_ref[...]
    put_words(slots_ref, 0, (donors // 8) * 24 + donors % 8)
    targets = targets_ref[...]
    put_words(slots_ref, 4, jnp.where(targets >= 0, (targets // 8) * 24 + targets % 8, STATE_ROWS))


def place_kernel(state_ref, arrived_ref, slots_ref, new_ref, low_ref, high_ref):
    new_ref[...] = state_ref[...]

    def body(block, carry):
        for s in range(8):
            put_row(new_ref, slots_ref[SLOTS + block * 8 + s], row(arrived_ref, block * 24 + s))
        return carry

    lax.fori_loop(0, SLOTS // 8, body, 0)
    for first, out in ((0, low_ref), (ELEMS - HALO, high_ref)):
        value = new_ref[first * 3 : (first + HALO) * 3, :].reshape(HALO // 8, 3, 8, LANES)
        out[0:256, :] = value[:, 0].reshape(HALO, LANES)
        out[256:512, :] = value[:, 1].reshape(HALO, LANES)
        last = value[:, 2].reshape(HALO, LANES)
        out[512:640, :] = last[0:128] + pltpu.roll(last[128:256], 64, 1)


def local_kernel(state_ref, matrix_ref, where_hbm, own_ref, gathered_ref, x, table, where_ref, sem):
    copy = pltpu.make_async_copy(where_hbm, where_ref, sem)
    copy.start()
    fill_operand(x, columns_of(state_ref))
    multiply(x, matrix_ref, ELEMS, LOCAL_PAIR, table, own_ref)
    copy.wait()

    def body(block, carry):
        gather_group(table, where_ref, block, gathered_ref)
        return carry

    lax.fori_loop(0, ELEMS // 8, body, 0)


def total(own_ref, gathered_ref, low_ref, high_ref, matrix_ref, where_hbm, active_ref, x, table, more, where_ref, sem):
    copy = pltpu.make_async_copy(where_hbm, where_ref, sem)
    copy.start()
    lane = lax.broadcasted_iota(jnp.int32, (128, LANES), 1)
    columns = []
    for c in range(2):
        rows = slice(c * 256, (c + 1) * 256)
        columns.append(jnp.concatenate([low_ref[rows, :], high_ref[rows, :]], axis=0))
    last = []
    for ref in (low_ref, high_ref):
        both = ref[512:640, :]
        last.append(jnp.where(lane < 64, both, 0.0))
        last.append(jnp.where(lane < 64, pltpu.roll(both, 64, 1), 0.0))
    columns.append(jnp.concatenate(last, axis=0))
    fill_operand(x, columns)
    multiply(x, matrix_ref, 2 * HALO, HALO_PAIR, table, None)
    copy.wait()

    def body(block, carry):
        @pl.when(active_ref[block] > 0)
        def _():
            gather_group(table, where_ref, block, more)

        @pl.when(active_ref[block] <= 0)
        def _():
            more[pl.ds(pl.multiple_of(block * 64, 8), 64), :] = jnp.zeros((64, LANES), jnp.float32)

        return carry

    lax.fori_loop(0, ELEMS // 8, body, 0)
    return [a + b + c for a, b, c in zip(columns_of(own_ref), join(gathered_ref), join(more))]


def middle_kernel(
    state_ref, own_ref, gathered_ref, low_ref, high_ref, matrix_ref, where_hbm, active_ref, factor_ref,
    slots_ref, choose_ref, patterns_ref,
    new_ref, out_ref,
    x, table, more, where_ref, sem, picked, operand,
):
    sums = total(
        own_ref, gathered_ref, low_ref, high_ref, matrix_ref, where_hbm, active_ref, x, table, more, where_ref, sem
    )
    factor = factor_ref[...]
    put_columns(new_ref, [w + factor * a for w, a in zip(columns_of(state_ref), sums)])
    new_ref[STATE_ROWS:, :] = jnp.zeros((PAD_ROWS, LANES), jnp.float32)
    send_blocks(new_ref, slots_ref, choose_ref, patterns_ref, out_ref, picked, operand)


def last_kernel(
    first_ref, state_ref, own_ref, gathered_ref, low_ref, high_ref, matrix_ref, where_hbm, active_ref,
    factor_ref,
    out_ref,
    x, table, more, where_ref, sem,
):
    sums = total(
        own_ref, gathered_ref, low_ref, high_ref, matrix_ref, where_hbm, active_ref, x, table, more, where_ref, sem
    )
    factor = factor_ref[...]
    for c, (f, w, a) in enumerate(zip(columns_of(first_ref), columns_of(state_ref), sums)):
        result = 0.5 * f + 0.5 * (w + factor * a)
        turned = result.T
        if c < 2:
            out_ref[c * LANES : (c + 1) * LANES, :] = turned
        else:
            out_ref[256:320, :] = turned[0:64]


def estimate(flops, size):
    return pl.CostEstimate(flops=flops, bytes_accessed=size, transcendentals=0)


STATE = (STATE_ROWS + PAD_ROWS, LANES)
MESSAGE = (MESSAGE_ROWS, LANES)
RIM = (640, LANES)


def near(shape, dtype=jnp.float32):
    return pltpu.VMEM(shape, dtype)


def held(value):
    return pltpu.with_memory_space_constraint(value, pltpu.VMEM)


def call(kernel, name, outs, specs, scratch, cost, *args):
    args = [held(a) if spec is VMEM_HELD else a for a, spec in zip(args, specs)]
    return pl.pallas_call(
        kernel,
        out_shape=outs,
        in_specs=[VMEM if spec is VMEM_HELD else spec for spec in specs],
        out_specs=jax.tree.map(lambda _: VMEM, outs) if not isinstance(outs, tuple) else tuple(VMEM for _ in outs),
        scratch_shapes=scratch,
        compiler_params=pltpu.CompilerParams(vmem_limit_bytes=VMEM_LIMIT),
        cost_estimate=cost,
        name=name,
    )(*args)


VMEM_HELD = object()
H = VMEM_HELD


def sum_scratch(count, pair_rows):
    return [
        pltpu.VMEM((count, 1024), jnp.bfloat16),
        pltpu.VMEM((3 * pair_rows * 8, LANES), jnp.float32),
    ]


WHERE_SCRATCH = [pltpu.SMEM((6 * ELEMS,), jnp.int32), pltpu.SemaphoreType.DMA(())]
HALO_SCRATCH = sum_scratch(2 * HALO, HALO_PAIR) + [pltpu.VMEM((ELEMS * 8, LANES), jnp.float32)] + WHERE_SCRATCH
SEND_SCRATCH = [
    pltpu.VMEM((MESSAGE_ROWS + 8, LANES), jnp.float32),
    pltpu.VMEM((MESSAGE_ROWS, 3 * LANES), jnp.bfloat16),
]


def words(rows):
    return jax.ShapeDtypeStruct((rows, LANES), jnp.int32)


def swap(message):
    return lax.ppermute(message, "sec", [(0, 1), (1, 0)])


def spread(crossed):
    blocks = crossed.reshape(64, MESSAGE_ROWS // 64, LANES)
    return lax.all_to_all(blocks, "elem", 0, 0, tiled=True).reshape(MESSAGE_ROWS, LANES)


def rims(low, high):
    count = lax.axis_size("elem")
    up = [(i, i + 1) for i in range(count - 1)]
    down = [(i + 1, i) for i in range(count - 1)]
    return lax.ppermute(high, "elem", up), lax.ppermute(low, "elem", down)


def local(
    fields,
    jacobian,
    face_links,
    volume_matrix,
    face_matrices,
    patterns,
    donor_index,
    pattern_index,
    receivers,
):
    message = call(
        start_kernel, "start", near(MESSAGE), [VMEM] * 4,
        [pltpu.VMEM((640, ELEMS), jnp.bfloat16), pltpu.VMEM((ELEMS, SLOTS), jnp.bfloat16)],
        estimate(10**9, 2 * 10**6),
        fields[0], donor_index, pattern_index, patterns,
    )
    crossed = swap(message)
    arrived = spread(crossed)
    state, factor, matrix, pattern_blocks, choose, local_rows, rim_rows, active, slots = call(
        prepare_kernel, "prepare",
        (
            near(STATE), near((ELEMS, LANES)), near((1024, PRODUCT_TILES * LANES), jnp.bfloat16),
            near((3 * LANES, NPAT * LANES), jnp.bfloat16), near((SLOTS, LANES), jnp.int32),
            words(48), words(48), words(8), words(8),
        ),
        [VMEM] * 9 + [ANY], [], estimate(2 * 10**10, 40 * 10**6),
        fields[0], jacobian, face_links[0], volume_matrix[0], face_matrices[0], patterns, donor_index,
        pattern_index, receivers, crossed,
    )
    local_rows, rim_rows, active, slots = [v.reshape(-1) for v in (local_rows, rim_rows, active, slots)]

    def settle(values, arrived):
        return call(
            place_kernel, "place", (near(STATE), near(RIM), near(RIM)), [H, H, SMEM], [],
            estimate(10**6, 4 * 10**6), values, arrived, slots,
        )

    def local_sum(values):
        return call(
            local_kernel, "local_sum", (near((STATE_ROWS, LANES)), near((ELEMS * 8, LANES))), [H, H, ANY],
            sum_scratch(ELEMS, LOCAL_PAIR) + WHERE_SCRATCH, estimate(10**10, 30 * 10**6),
            values, matrix, local_rows,
        )

    first, low, high = settle(state, arrived)
    below, above = rims(low, high)
    own, gathered = local_sum(first)
    middle, message = call(
        middle_kernel, "middle_step", (near(STATE), near(MESSAGE)),
        [H] * 6 + [ANY, SMEM, H, SMEM, H, H], HALO_SCRATCH + SEND_SCRATCH, estimate(6 * 10**9, 10**7),
        first, own, gathered, below, above, matrix, rim_rows, active, factor, slots, choose, pattern_blocks,
    )
    arrived = spread(swap(message))
    second, low, high = settle(middle, arrived)
    below, above = rims(low, high)
    own, gathered = local_sum(second)
    advanced = call(
        last_kernel, "last_step", jax.ShapeDtypeStruct((320, ELEMS), jnp.float32),
        [H] * 7 + [ANY, SMEM, H], HALO_SCRATCH, estimate(6 * 10**9, 10**7),
        first, second, own, gathered, below, above, matrix, rim_rows, active, factor,
    )
    return advanced[None]


def solution(mesh):
    return jax.shard_map(
        local,
        mesh=mesh,
        in_specs=(
            P("sec", None, "elem"),
            P("sec", "elem"),
            P("sec", None, "elem"),
            P("sec", None, None),
            P("sec", None, None, None),
            P(),
            P("sec", "elem"),
            P("sec", "elem"),
            P("sec", "elem"),
        ),
        out_specs=P("sec", None, "elem"),
        check_vma=False,
    )
```

```python
import jax
import jax.numpy as jnp
from jax import lax
from jax.experimental import pallas as pl
from jax.experimental.pallas import tpu as pltpu
from jax.sharding import PartitionSpec as P

NPAT = 4
HALO = 256
ELEMS = 1024
SLOTS = 512
LANES = 128
STATE_ROWS = ELEMS * 3
PAD_ROWS = 24
MESSAGE_ROWS = SLOTS * 3
LOCAL_PAIR = ELEMS + 8
HALO_PAIR = 2 * HALO + 8
PRODUCT_TILES = 18
LIST = 400
VMEM_LIMIT = 28 * 1024 * 1024

VMEM = pl.BlockSpec(memory_space=pltpu.VMEM)
SMEM = pl.BlockSpec(memory_space=pltpu.SMEM)
ANY = pl.BlockSpec(memory_space=pl.ANY)
HBM = pl.BlockSpec(memory_space=pltpu.HBM)


def row(ref, start):
    return ref[pl.ds(start, 3, stride=8), :]


def put_row(ref, start, value):
    ref[pl.ds(start, 3, stride=8), :] = value


def tiles_of(value, count):
    return value.reshape(count // 8, 3, 8, LANES)


def split(value):
    high = value.astype(jnp.bfloat16).astype(jnp.float32)
    return high, value - high


def fill_operand(x_ref, columns):
    h0, l0 = split(columns[0])
    h1, l1 = split(columns[1])
    h2, l2 = split(columns[2])
    both = h2 + pltpu.roll(l2, 64, 1)
    for k, part in enumerate((h0, h1, l0, l1, h0, h1, both, h2)):
        x_ref[:, k * LANES : (k + 1) * LANES] = part.astype(jnp.bfloat16)


def put_tile(table, element, tile, block):
    for r in range(block.shape[0] // 8):
        start = pl.multiple_of((element + r * 8) * 8, 64)
        table[pl.ds(start + tile, 8, stride=8), :] = block[r * 8 : r * 8 + 8]


def even_rows():
    sub = lax.broadcasted_iota(jnp.int32, (8, LANES), 0)
    lane = lax.broadcasted_iota(jnp.int32, (8, LANES), 1)
    return (sub < 2) | ((sub == 2) & (lane < 64))


def tile_at(table, place):
    return table[pl.ds(pl.multiple_of(place, 8), 8), :]


def clear_tile(table, element):
    table[pl.ds(element * 8, 8), :] = jnp.zeros((8, LANES), jnp.float32)


def join(ref):
    part = [ref[pl.ds(c, ELEMS, stride=8), :] for c in range(5)]
    lane = lax.broadcasted_iota(jnp.int32, (ELEMS, LANES), 1)
    last = jnp.where(lane < 64, part[2] + pltpu.roll(part[2], 64, 1), 0.0)
    return part[0] + part[3], part[1] + part[4], last


def columns_of(ref):
    value = tiles_of(ref[0:STATE_ROWS, :], ELEMS)
    return [value[:, c].reshape(ELEMS, LANES) for c in range(3)]


def put_columns(ref, columns):
    stacked = jnp.stack([c.reshape(ELEMS // 8, 8, LANES) for c in columns], axis=1)
    ref[0:STATE_ROWS, :] = stacked.reshape(STATE_ROWS, LANES)


def send_blocks(state_ref, donors_ref, choose_ref, patterns_ref, out_ref, picked, operand):
    def body(block, carry):
        for s in range(8):
            put_row(picked, block * 24 + s, row(state_ref, donors_ref[block * 8 + s]))
        return carry

    lax.fori_loop(0, SLOTS // 8, body, 0)
    high, low = split(picked[0:MESSAGE_ROWS])
    for k, part in enumerate((high, low, high)):
        operand[:, k * LANES : (k + 1) * LANES] = part.astype(jnp.bfloat16)
    mapped = jnp.dot(operand[...], patterns_ref[...], preferred_element_type=jnp.float32)
    choose = down(choose_ref, SLOTS).reshape(SLOTS // 8, 1, 8, LANES)
    result = tiles_of(mapped[:, :LANES], SLOTS)
    for which in range(1, NPAT):
        other = tiles_of(mapped[:, which * LANES : (which + 1) * LANES], SLOTS)
        result = jnp.where(choose == which, other, result)
    out_ref[...] = result.reshape(MESSAGE_ROWS, LANES)


def start_kernel(
    fields_hbm, donors_hbm, choose_hbm, patterns_hbm, out_ref,
    both, chosen, fields_ref, donors_ref, choose_ref, patterns_ref, sems,
):
    pairs = (
        (donors_hbm, donors_ref), (choose_hbm, choose_ref), (patterns_hbm, patterns_ref), (fields_hbm, fields_ref)
    )
    copies = [pltpu.make_async_copy(a, b, sems.at[k]) for k, (a, b) in enumerate(pairs)]
    for copy in copies:
        copy.start()
    copies[0].wait()
    element = lax.broadcasted_iota(jnp.int32, (ELEMS, SLOTS), 0)
    chosen[...] = (element == donors_ref[...]).astype(jnp.float32).astype(jnp.bfloat16)
    for copy in copies[1:]:
        copy.wait()
    high, low = split(fields_ref[...])
    both[0:320, :] = high.astype(jnp.bfloat16)
    both[320:640, :] = low.astype(jnp.bfloat16)
    picked = jnp.dot(both[...], chosen[...], preferred_element_type=jnp.float32)
    high = picked[0:320].astype(jnp.bfloat16)
    low = picked[320:640].astype(jnp.bfloat16)
    patterns_high, patterns_low = split(patterns_ref[...].reshape(NPAT * 64, 64))
    weights = jnp.concatenate([patterns_high, patterns_high, patterns_low], axis=1).astype(jnp.bfloat16)
    which = choose_ref[...]
    results = []
    for v in range(5):
        rows = slice(v * 64, (v + 1) * 64)
        operand = jnp.concatenate([high[rows], low[rows], high[rows]], axis=0)
        mapped = jnp.dot(weights, operand, preferred_element_type=jnp.float32)
        result = mapped[0:64]
        for p in range(1, NPAT):
            result = jnp.where(which == p, mapped[p * 64 : (p + 1) * 64], result)
        results.append(result)
    results.append(jnp.zeros((64, SLOTS), jnp.float32))
    for c in range(3):
        tall = jnp.concatenate([results[2 * c], results[2 * c + 1]], axis=0)
        for block in range(SLOTS // LANES):
            turned = tall[:, block * LANES : (block + 1) * LANES].T
            for r in range(16):
                out_ref[pl.ds((block * 16 + r) * 24 + c * 8, 8), :] = turned[r * 8 : r * 8 + 8]


def down(ref, count):
    columns = []
    for block in range(count // LANES):
        value = ref[:, block * LANES : (block + 1) * LANES].astype(jnp.float32)
        columns.append(jnp.broadcast_to(value, (LANES, LANES)).T)
    return jnp.concatenate(columns, axis=0)


def turn(piece):
    missing = LANES - piece.shape[0], LANES - piece.shape[1]
    if missing[1]:
        piece = jnp.concatenate([piece, jnp.zeros((piece.shape[0], missing[1]), jnp.float32)], axis=1)
    if missing[0]:
        piece = jnp.concatenate([piece, jnp.zeros((missing[0], LANES), jnp.float32)], axis=0)
    return piece.T


def put_words(out_ref, first, value):
    for k in range(value.shape[1] // LANES):
        out_ref[first + k : first + k + 1, :] = value[:, k * LANES : (k + 1) * LANES]


def prepare_kernel(
    fields_hbm, links_ref, volume_hbm, faces_hbm, patterns_ref, donors_ref, targets_ref, after_ref,
    state_ref, matrix_ref, patterns_out,
    local_ref, rim_ref, slots_ref, active_ref,
    counted, flags, fields_ref, volume_ref, faces_ref, sem, sems,
):
    del after_ref
    pairs = ((fields_hbm, fields_ref), (volume_hbm, volume_ref), (faces_hbm, faces_ref))
    copies = [pltpu.make_async_copy(a, b, sems.at[k]) for k, (a, b) in enumerate(pairs)]
    for copy in copies:
        copy.start()
    outside = []
    is_odd = lax.axis_index("elem") % 2
    for face in range(6):
        links = links_ref[face : face + 1, :]
        own = (links >= HALO) & (links < HALO + ELEMS)
        pair = face // 2
        put_words(local_ref, face * 8, jnp.where(own, links - HALO, ELEMS) * 8)
        rim = jnp.where(links < HALO, links + HALO * (1 - is_odd), links - (HALO + ELEMS) + HALO * is_odd)
        put_words(rim_ref, face * 8, (jnp.where(own, 2 * HALO, rim) + pair * HALO_PAIR) * 8)
        outside.append(jnp.where(own, 0.0, 1.0))
    group = lax.broadcasted_iota(jnp.int32, (ELEMS, LANES), 0) // GROUP
    member = (group == lax.broadcasted_iota(jnp.int32, (ELEMS, LANES), 1)).astype(jnp.float32)
    outside = jnp.concatenate(outside + outside[:2], axis=0).astype(jnp.bfloat16)
    counted[...] = jnp.dot(
        outside, member.astype(jnp.bfloat16), preferred_element_type=jnp.float32
    ).astype(jnp.int32)
    copy = pltpu.make_async_copy(counted, flags, sem)
    copy.start()
    copy.wait()

    def note(block, counts):
        counts = list(counts)
        for face in range(6):
            parity = face % 2
            active_ref[parity * LIST + counts[parity]] = face * ELEMS + block * GROUP
            counts[parity] = counts[parity] + jnp.where(flags[face, block] > 0, 1, 0)
        return tuple(counts)

    zero = jnp.zeros((), jnp.int32)
    counts = lax.fori_loop(0, ELEMS // GROUP, note, (zero, zero))
    active_ref[2 * LIST] = counts[0]
    active_ref[2 * LIST + 1] = counts[1]
    donors = donors_ref[...]
    put_words(slots_ref, 0, (donors // 8) * 24 + donors % 8)
    targets = targets_ref[...]
    put_words(slots_ref, 4, jnp.where(targets >= 0, (targets // 8) * 24 + targets % 8, STATE_ROWS))
    for copy in copies:
        copy.wait()
    state_ref[STATE_ROWS:, :] = jnp.zeros((PAD_ROWS, LANES), jnp.float32)
    for block in range(ELEMS // LANES):
        lanes = slice(block * LANES, (block + 1) * LANES)
        for c in range(3):
            turned = turn(fields_ref[c * LANES : min((c + 1) * LANES, 320), lanes])
            for r in range(16):
                state_ref[pl.ds((block * 16 + r) * 24 + c * 8, 8), :] = turned[r * 8 : r * 8 + 8]
    for tile in range(PRODUCT_TILES):
        pair, kind = tile // 5, tile % 5
        columns = []
        for c in range(3):
            lanes = slice(c * LANES, min((c + 1) * LANES, 320))
            if tile >= 15:
                rows = slice((tile - 15) * LANES, min((tile - 14) * LANES, 320))
                piece = volume_ref[rows, lanes]
            elif kind == 2:
                piece = jnp.concatenate(
                    [faces_ref[2 * pair, 256:320, lanes], faces_ref[2 * pair + 1, 256:320, lanes]], axis=0
                )
            elif kind < 2:
                piece = faces_ref[2 * pair, kind * LANES : (kind + 1) * LANES, lanes]
            else:
                piece = faces_ref[2 * pair + 1, (kind - 3) * LANES : (kind - 2) * LANES, lanes]
            columns.append(turn(piece))
        h0, l0 = split(columns[0])
        h1, l1 = split(columns[1])
        h2, l2 = split(columns[2])
        twice = jnp.concatenate([h2[0:64], h2[0:64]], axis=0)
        at = slice(tile % 2 * LANES, (tile % 2 + 1) * LANES)
        for k, part in enumerate((h0, h1, h0, h1, l0, l1, twice, l2)):
            matrix_ref[tile // 2, k * LANES : (k + 1) * LANES, at] = part.astype(jnp.bfloat16)
    zero = jnp.zeros((64, 64), jnp.float32)
    for which in range(NPAT):
        one = patterns_ref[which]
        block = jnp.concatenate(
            [jnp.concatenate([one, zero], axis=1), jnp.concatenate([zero, one], axis=1)], axis=0
        )
        high, low = split(block.T)
        at = slice(which * LANES, (which + 1) * LANES)
        for k, part in enumerate((high, high, low)):
            patterns_out[k * LANES : (k + 1) * LANES, at] = part.astype(jnp.bfloat16)


def place_kernel(state_ref, arrived_ref, slots_ref, new_ref, near_ref, far_ref):
    new_ref[...] = state_ref[...]

    def body(block, carry):
        for s in range(8):
            put_row(new_ref, slots_ref[SLOTS + block * 8 + s], row(arrived_ref, block * 24 + s))
        return carry

    lax.fori_loop(0, SLOTS // 8, body, 0)
    is_odd = lax.axis_index("elem") % 2
    top = 3 * (ELEMS - HALO)
    for first, out in ((top * (1 - is_odd), near_ref), (top * is_odd, far_ref)):
        value = new_ref[pl.ds(pl.multiple_of(first, 8), 3 * HALO), :].reshape(HALO // 8, 3, 8, LANES)
        out[0:256, :] = value[:, 0].reshape(HALO, LANES)
        out[256:512, :] = value[:, 1].reshape(HALO, LANES)
        last = value[:, 2].reshape(HALO, LANES)
        out[512:640, :] = last[0:128] + pltpu.roll(last[128:256], 64, 1)


GROUP = 16


def gather_pair(table, where_ref, pair, first, count, out_ref):
    values = []
    for k in range(count):
        g = first + k
        even = tile_at(table, where_ref[2 * pair * ELEMS + g])
        odd = tile_at(table, where_ref[(2 * pair + 1) * ELEMS + g])
        value = jnp.where(even_rows(), even, odd)
        if pair > 0:
            value = value + tile_at(out_ref, g * 8)
        values.append(value)
    for k in range(count):
        out_ref[pl.ds(pl.multiple_of((first + k) * 8, 8), 8), :] = values[k]


def local_kernel(
    state_ref, matrix_hbm, where_hbm, own_ref, gathered_ref, x, w, table0, table1, table2, where_ref, sem, sems
):
    copies = []
    for k in range(3):
        third = pl.ds(3 * k, 3)
        copies.append(pltpu.make_async_copy(matrix_hbm.at[third], w.at[third], sems.at[k]))
    copies[0].start()
    copy = pltpu.make_async_copy(where_hbm, where_ref, sem)
    copy.start()
    fill_operand(x, columns_of(state_ref))
    tables = (table0, table1, table2)
    for table in tables:
        clear_tile(table, ELEMS)
    groups = ELEMS // GROUP
    for n in range(9):
        if n % 3 == 0:
            copies[n // 3].wait()
        if n == 0:
            copies[1].start()
            copies[2].start()
        product = jnp.dot(x[...], w[n], preferred_element_type=jnp.float32)
        for half in range(2):
            tile = 2 * n + half
            block = product[:, half * LANES : (half + 1) * LANES]
            if tile < 15:
                put_tile(tables[tile // 5], 0, tile % 5, block)
            else:
                for r in range(ELEMS // 8):
                    own_ref[pl.ds(r * 24 + (tile - 15) * 8, 8), :] = block[r * 8 : r * 8 + 8]
        if n == 2:
            copy.wait()
        if n >= 3:
            part = n % 3
            for k in range(groups * part // 3, groups * (part + 1) // 3):
                gather_pair(tables[n // 3 - 1], where_ref, n // 3 - 1, k * GROUP, GROUP, gathered_ref)

    def body(k, carry):
        gather_pair(table2, where_ref, 2, k * GROUP, GROUP, gathered_ref)
        return carry

    lax.fori_loop(0, groups, body, 0)


def total(
    own_ref, gathered_ref, near_ref, far_ref, w, where_hbm, active_hbm, sums_ref, x, table, where_ref, active_ref,
    sems,
):
    del gathered_ref
    copies = [
        pltpu.make_async_copy(where_hbm, where_ref, sems.at[0]),
        pltpu.make_async_copy(active_hbm, active_ref, sems.at[1]),
    ]
    for copy in copies:
        copy.start()
    lane = lax.broadcasted_iota(jnp.int32, (128, LANES), 1)
    columns = []
    for c in range(2):
        rows = slice(c * 256, (c + 1) * 256)
        columns.append(jnp.concatenate([near_ref[rows, :], far_ref[rows, :]], axis=0))
    last = []
    for ref in (near_ref, far_ref):
        both = ref[512:640, :]
        last.append(jnp.where(lane < 64, both, 0.0))
        last.append(jnp.where(lane < 64, pltpu.roll(both, 64, 1), 0.0))
    columns.append(jnp.concatenate(last, axis=0))
    fill_operand(x, columns)
    for pair in range(3):
        clear_tile(table, pair * HALO_PAIR + 2 * HALO)
    for n in range(8):
        product = jnp.dot(x[...], w[n], preferred_element_type=jnp.float32)
        for half in range(2):
            tile = 2 * n + half
            if tile < 15:
                put_tile(table, (tile // 5) * HALO_PAIR, tile % 5, product[:, half * LANES : (half + 1) * LANES])
    for copy in copies:
        copy.wait()
    for parity in range(2):

        def body(k, carry, parity=parity):
            first = active_ref[parity * LIST + k]
            g = first & (ELEMS - 1)
            values = []
            for s in range(GROUP):
                value = tile_at(table, where_ref[first + s])
                value = jnp.where(even_rows() if parity == 0 else ~even_rows(), value, 0.0)
                values.append(tile_at(sums_ref, (g + s) * 8) + value)
            for s in range(GROUP):
                sums_ref[pl.ds(pl.multiple_of((g + s) * 8, 8), 8), :] = values[s]
            return carry

        lax.fori_loop(0, active_ref[2 * LIST + parity], body, 0)
    return [a + b for a, b in zip(columns_of(own_ref), join(sums_ref))]


def middle_kernel(
    state_ref, own_ref, gathered_ref, near_ref, far_ref, w, where_hbm, active_hbm, jacobian_ref,
    slots_hbm, choose_ref, patterns_ref,
    new_ref, out_ref, sums_ref,
    x, table, where_ref, active_ref, sems, picked, operand, slots_ref, sem,
):
    copy = pltpu.make_async_copy(slots_hbm, slots_ref, sem)
    copy.start()
    sums = total(
        own_ref, gathered_ref, near_ref, far_ref, w, where_hbm, active_hbm, sums_ref, x, table, where_ref,
        active_ref, sems,
    )
    factor = 0.25 * down(jacobian_ref, ELEMS)
    put_columns(new_ref, [w + factor * a for w, a in zip(columns_of(state_ref), sums)])
    new_ref[STATE_ROWS:, :] = jnp.zeros((PAD_ROWS, LANES), jnp.float32)
    copy.wait()
    send_blocks(new_ref, slots_ref, choose_ref, patterns_ref, out_ref, picked, operand)


def last_kernel(
    first_ref, state_ref, own_ref, gathered_ref, near_ref, far_ref, w, where_hbm, active_hbm,
    jacobian_ref,
    out_ref, sums_ref,
    x, table, where_ref, active_ref, sems,
):
    sums = total(
        own_ref, gathered_ref, near_ref, far_ref, w, where_hbm, active_hbm, sums_ref, x, table, where_ref,
        active_ref, sems,
    )
    factor = 0.25 * down(jacobian_ref, ELEMS)
    for c, (f, w, a) in enumerate(zip(columns_of(first_ref), columns_of(state_ref), sums)):
        result = 0.5 * f + 0.5 * (w + factor * a)
        turned = result.T
        if c < 2:
            out_ref[c * LANES : (c + 1) * LANES, :] = turned
        else:
            out_ref[256:320, :] = turned[0:64]


def estimate(flops, size):
    return pl.CostEstimate(flops=flops, bytes_accessed=size, transcendentals=0)


STATE = (STATE_ROWS + PAD_ROWS, LANES)
MESSAGE = (MESSAGE_ROWS, LANES)
RIM = (640, LANES)
GATHERED = (ELEMS * 8, LANES)


def near(shape, dtype=jnp.float32):
    return pltpu.VMEM(shape, dtype)


def held(value):
    return pltpu.with_memory_space_constraint(value, pltpu.VMEM)


def call(kernel, name, outs, specs, scratch, cost, *args, aliases=None, out_specs=None):
    args = [held(a) if spec is VMEM_HELD else a for a, spec in zip(args, specs)]
    return pl.pallas_call(
        kernel,
        out_shape=outs,
        in_specs=[VMEM if spec is VMEM_HELD else spec for spec in specs],
        out_specs=out_specs or (tuple(VMEM for _ in outs) if isinstance(outs, tuple) else VMEM),
        input_output_aliases=aliases or {},
        scratch_shapes=scratch,
        compiler_params=pltpu.CompilerParams(vmem_limit_bytes=VMEM_LIMIT),
        cost_estimate=cost,
        name=name,
    )(*args)


VMEM_HELD = object()
H = VMEM_HELD


def near_scratch(*shape, dtype=jnp.float32):
    return pltpu.VMEM(shape, dtype)


LOCAL_SCRATCH = (
    [near_scratch(ELEMS, 1024, dtype=jnp.bfloat16), near_scratch(9, 1024, 256, dtype=jnp.bfloat16)]
    + [near_scratch(LOCAL_PAIR * 8, LANES)] * 3
    + [pltpu.SMEM((6 * ELEMS,), jnp.int32), pltpu.SemaphoreType.DMA(()), pltpu.SemaphoreType.DMA((3,))]
)
HALO_SCRATCH = [
    near_scratch(2 * HALO, 1024, dtype=jnp.bfloat16), near_scratch(3 * HALO_PAIR * 8, LANES),
    pltpu.SMEM((6 * ELEMS,), jnp.int32), pltpu.SMEM((1024,), jnp.int32), pltpu.SemaphoreType.DMA((2,)),
]
SEND_SCRATCH = [
    pltpu.VMEM((MESSAGE_ROWS + 8, LANES), jnp.float32),
    pltpu.VMEM((MESSAGE_ROWS, 3 * LANES), jnp.bfloat16),
    pltpu.SMEM((1024,), jnp.int32), pltpu.SemaphoreType.DMA(()),
]


def words(rows):
    return jax.ShapeDtypeStruct((rows, LANES), jnp.int32)


def swap(message):
    return lax.ppermute(message, "sec", [(0, 1), (1, 0)])


def spread(crossed):
    blocks = crossed.reshape(64, MESSAGE_ROWS // 64, LANES)
    return lax.all_to_all(blocks, "elem", 0, 0, tiled=True).reshape(MESSAGE_ROWS, LANES)


def rims(near_rim, far_rim):
    count = lax.axis_size("elem")

    def swaps(first):
        pairs = [(i, i + 1) for i in range(first, count - 1, 2)]
        return pairs + [(b, a) for a, b in pairs]

    return lax.ppermute(near_rim, "elem", swaps(0)), lax.ppermute(far_rim, "elem", swaps(1))


def local(
    fields,
    jacobian,
    face_links,
    volume_matrix,
    face_matrices,
    patterns,
    donor_index,
    pattern_index,
    receivers,
):
    message = call(
        start_kernel, "start", near(MESSAGE), [HBM] * 4,
        [
            pltpu.VMEM((640, ELEMS), jnp.bfloat16), pltpu.VMEM((ELEMS, SLOTS), jnp.bfloat16),
            pltpu.VMEM((320, ELEMS), jnp.float32), pltpu.VMEM((1, SLOTS), jnp.int32),
            pltpu.VMEM((1, SLOTS), jnp.int32), pltpu.VMEM((NPAT, 64, 64), jnp.float32),
            pltpu.SemaphoreType.DMA((4,)),
        ],
        estimate(10**9, 2 * 10**6),
        *[pltpu.with_memory_space_constraint(v, pltpu.HBM) for v in (fields[0], donor_index, pattern_index, patterns)],
    )
    crossed = swap(message)
    arrived = spread(crossed)
    far = [pltpu.with_memory_space_constraint(v, pltpu.HBM) for v in (fields[0], volume_matrix[0], face_matrices[0])]
    state, matrix, pattern_blocks, local_rows, rim_rows, slots, active = call(
        prepare_kernel, "prepare",
        (
            near(STATE), near((9, 1024, 256), jnp.bfloat16), near((3 * LANES, NPAT * LANES), jnp.bfloat16),
            words(48), words(48), words(8), jax.ShapeDtypeStruct((1024,), jnp.int32),
        ),
        [HBM, VMEM, HBM, HBM] + [VMEM] * 3 + [ANY],
        [
            pltpu.VMEM((8, LANES), jnp.int32), pltpu.SMEM((8, LANES), jnp.int32),
            near_scratch(320, ELEMS), near_scratch(320, 320), near_scratch(6, 320, 320),
            pltpu.SemaphoreType.DMA(()), pltpu.SemaphoreType.DMA((3,)),
        ],
        estimate(2 * 10**10, 40 * 10**6),
        far[0], face_links[0], far[1], far[2], patterns, donor_index, receivers, crossed,
        out_specs=(VMEM,) * 6 + (SMEM,),
    )
    local_rows, rim_rows, slots = [v.reshape(-1) for v in (local_rows, rim_rows, slots)]

    def settle(values, arrived):
        return call(
            place_kernel, "place", (near(STATE), near(RIM), near(RIM)), [H, H, SMEM], [],
            estimate(10**6, 4 * 10**6), values, arrived, slots,
        )

    def local_sum(values):
        return call(
            local_kernel, "local_sum", (near((STATE_ROWS, LANES)), near(GATHERED)), [H, HBM, ANY],
            LOCAL_SCRATCH, estimate(10**10, 30 * 10**6),
            values, pltpu.with_memory_space_constraint(matrix, pltpu.HBM), local_rows,
        )

    first, near_rim, far_rim = settle(state, arrived)
    near_got, far_got = rims(near_rim, far_rim)
    own, gathered = local_sum(first)
    middle, message, _ = call(
        middle_kernel, "middle_step", (near(STATE), near(MESSAGE), near(GATHERED)),
        [H] * 6 + [ANY, ANY, VMEM, ANY, VMEM, H], HALO_SCRATCH + SEND_SCRATCH, estimate(6 * 10**9, 10**7),
        first, own, gathered, near_got, far_got, matrix, rim_rows, active, jacobian, slots, pattern_index, pattern_blocks,
        aliases={2: 2},
    )
    arrived = spread(swap(message))
    second, near_rim, far_rim = settle(middle, arrived)
    near_got, far_got = rims(near_rim, far_rim)
    own, gathered = local_sum(second)
    advanced, _ = call(
        last_kernel, "last_step", (jax.ShapeDtypeStruct((320, ELEMS), jnp.float32), near(GATHERED)),
        [H] * 7 + [ANY, ANY, VMEM], HALO_SCRATCH, estimate(6 * 10**9, 10**7),
        first, second, own, gathered, near_got, far_got, matrix, rim_rows, active, jacobian,
        aliases={3: 1},
    )
    return advanced[None]


def solution(mesh):
    return jax.shard_map(
        local,
        mesh=mesh,
        in_specs=(
            P("sec", None, "elem"),
            P("sec", "elem"),
            P("sec", None, "elem"),
            P("sec", None, None),
            P("sec", None, None, None),
            P(),
            P("sec", "elem"),
            P("sec", "elem"),
            P("sec", "elem"),
        ),
        out_specs=P("sec", None, "elem"),
        check_vma=False,
    )
```

```python
import jax
import jax.numpy as jnp
from jax import lax
from jax.experimental import pallas as pl
from jax.experimental.pallas import tpu as pltpu
from jax.sharding import PartitionSpec as P

NPAT = 4
HALO = 256
ELEMS = 1024
SLOTS = 512
LANES = 128
STATE_ROWS = ELEMS * 3
PAD_ROWS = 24
MESSAGE_ROWS = SLOTS * 3
LOCAL_PAIR = ELEMS + 8
HALO_PAIR = 2 * HALO + 8
PRODUCT_TILES = 18
LIST = 400
VMEM_LIMIT = 28 * 1024 * 1024

VMEM = pl.BlockSpec(memory_space=pltpu.VMEM)
SMEM = pl.BlockSpec(memory_space=pltpu.SMEM)
ANY = pl.BlockSpec(memory_space=pl.ANY)
HBM = pl.BlockSpec(memory_space=pltpu.HBM)


def row(ref, start):
    return ref[pl.ds(start, 3, stride=8), :]


def put_row(ref, start, value):
    ref[pl.ds(start, 3, stride=8), :] = value


def tiles_of(value, count):
    return value.reshape(count // 8, 3, 8, LANES)


def split(value):
    high = value.astype(jnp.bfloat16).astype(jnp.float32)
    return high, value - high


def fill_operand(x_ref, columns):
    h0, l0 = split(columns[0])
    h1, l1 = split(columns[1])
    h2, l2 = split(columns[2])
    both = h2 + pltpu.roll(l2, 64, 1)
    for k, part in enumerate((h0, h1, l0, l1, h0, h1, both, h2)):
        x_ref[:, k * LANES : (k + 1) * LANES] = part.astype(jnp.bfloat16)


def put_tile(table, element, tile, block):
    for r in range(block.shape[0] // 8):
        start = pl.multiple_of((element + r * 8) * 8, 64)
        table[pl.ds(start + tile, 8, stride=8), :] = block[r * 8 : r * 8 + 8]


def even_rows():
    sub = lax.broadcasted_iota(jnp.int32, (8, LANES), 0)
    lane = lax.broadcasted_iota(jnp.int32, (8, LANES), 1)
    return (sub < 2) | ((sub == 2) & (lane < 64))


def tile_at(table, place):
    return table[pl.ds(pl.multiple_of(place, 8), 8), :]


def clear_tile(table, element):
    table[pl.ds(element * 8, 8), :] = jnp.zeros((8, LANES), jnp.float32)


def join(ref):
    part = [ref[pl.ds(c, ELEMS, stride=8), :] for c in range(5)]
    lane = lax.broadcasted_iota(jnp.int32, (ELEMS, LANES), 1)
    last = jnp.where(lane < 64, part[2] + pltpu.roll(part[2], 64, 1), 0.0)
    return part[0] + part[3], part[1] + part[4], last


def columns_of(ref):
    value = tiles_of(ref[0:STATE_ROWS, :], ELEMS)
    return [value[:, c].reshape(ELEMS, LANES) for c in range(3)]


def put_columns(ref, columns):
    stacked = jnp.stack([c.reshape(ELEMS // 8, 8, LANES) for c in columns], axis=1)
    ref[0:STATE_ROWS, :] = stacked.reshape(STATE_ROWS, LANES)


def send_blocks(state_ref, donors_ref, choose_ref, patterns_ref, out_ref, picked, operand):
    def body(block, carry):
        for s in range(8):
            put_row(picked, block * 24 + s, row(state_ref, donors_ref[block * 8 + s]))
        return carry

    lax.fori_loop(0, SLOTS // 8, body, 0)
    high, low = split(picked[0:MESSAGE_ROWS])
    for k, part in enumerate((high, low, high)):
        operand[:, k * LANES : (k + 1) * LANES] = part.astype(jnp.bfloat16)
    mapped = jnp.dot(operand[...], patterns_ref[...], preferred_element_type=jnp.float32)
    choose = down(choose_ref, SLOTS).reshape(SLOTS // 8, 1, 8, LANES)
    result = tiles_of(mapped[:, :LANES], SLOTS)
    for which in range(1, NPAT):
        other = tiles_of(mapped[:, which * LANES : (which + 1) * LANES], SLOTS)
        result = jnp.where(choose == which, other, result)
    out_ref[...] = result.reshape(MESSAGE_ROWS, LANES)


def start_kernel(
    fields_hbm, donors_hbm, choose_hbm, patterns_hbm, out_ref,
    both, chosen, fields_ref, donors_ref, choose_ref, patterns_ref, sems,
):
    pairs = (
        (donors_hbm, donors_ref), (choose_hbm, choose_ref), (patterns_hbm, patterns_ref), (fields_hbm, fields_ref)
    )
    copies = [pltpu.make_async_copy(a, b, sems.at[k]) for k, (a, b) in enumerate(pairs)]
    for copy in copies:
        copy.start()
    copies[0].wait()
    element = lax.broadcasted_iota(jnp.int32, (ELEMS, SLOTS), 0)
    chosen[...] = (element == donors_ref[...]).astype(jnp.float32).astype(jnp.bfloat16)
    for copy in copies[1:]:
        copy.wait()
    high, low = split(fields_ref[...])
    both[0:320, :] = high.astype(jnp.bfloat16)
    both[320:640, :] = low.astype(jnp.bfloat16)
    picked = jnp.dot(both[...], chosen[...], preferred_element_type=jnp.float32)
    high = picked[0:320].astype(jnp.bfloat16)
    low = picked[320:640].astype(jnp.bfloat16)
    patterns_high, patterns_low = split(patterns_ref[...].reshape(NPAT * 64, 64))
    weights = jnp.concatenate([patterns_high, patterns_high, patterns_low], axis=1).astype(jnp.bfloat16)
    which = choose_ref[...]
    results = []
    for v in range(5):
        rows = slice(v * 64, (v + 1) * 64)
        operand = jnp.concatenate([high[rows], low[rows], high[rows]], axis=0)
        mapped = jnp.dot(weights, operand, preferred_element_type=jnp.float32)
        result = mapped[0:64]
        for p in range(1, NPAT):
            result = jnp.where(which == p, mapped[p * 64 : (p + 1) * 64], result)
        results.append(result)
    results.append(jnp.zeros((64, SLOTS), jnp.float32))
    for c in range(3):
        tall = jnp.concatenate([results[2 * c], results[2 * c + 1]], axis=0)
        for block in range(SLOTS // LANES):
            turned = tall[:, block * LANES : (block + 1) * LANES].T
            for r in range(16):
                out_ref[pl.ds((block * 16 + r) * 24 + c * 8, 8), :] = turned[r * 8 : r * 8 + 8]


def down(ref, count):
    columns = []
    for block in range(count // LANES):
        value = ref[:, block * LANES : (block + 1) * LANES].astype(jnp.float32)
        columns.append(jnp.broadcast_to(value, (LANES, LANES)).T)
    return jnp.concatenate(columns, axis=0)


def turn(piece):
    missing = LANES - piece.shape[0], LANES - piece.shape[1]
    if missing[1]:
        piece = jnp.concatenate([piece, jnp.zeros((piece.shape[0], missing[1]), jnp.float32)], axis=1)
    if missing[0]:
        piece = jnp.concatenate([piece, jnp.zeros((missing[0], LANES), jnp.float32)], axis=0)
    return piece.T


def put_words(out_ref, first, value):
    for k in range(value.shape[1] // LANES):
        out_ref[first + k : first + k + 1, :] = value[:, k * LANES : (k + 1) * LANES]


def prepare_kernel(
    fields_hbm, links_ref, volume_hbm, faces_hbm, patterns_ref, donors_ref, targets_ref, after_ref,
    state_ref, matrix_ref, patterns_out,
    local_ref, rim_ref, slots_ref, active_ref,
    counted, flags, fields_ref, volume_ref, faces_ref, sem, sems,
):
    del after_ref
    pairs = ((fields_hbm, fields_ref), (volume_hbm, volume_ref), (faces_hbm, faces_ref))
    copies = [pltpu.make_async_copy(a, b, sems.at[k]) for k, (a, b) in enumerate(pairs)]
    for copy in copies:
        copy.start()
    outside = []
    is_odd = lax.axis_index("elem") % 2
    for face in range(6):
        links = links_ref[face : face + 1, :]
        own = (links >= HALO) & (links < HALO + ELEMS)
        pair = face // 2
        put_words(local_ref, face * 8, jnp.where(own, links - HALO, ELEMS) * 8)
        rim = jnp.where(links < HALO, links + HALO * (1 - is_odd), links - (HALO + ELEMS) + HALO * is_odd)
        put_words(rim_ref, face * 8, (jnp.where(own, 2 * HALO, rim) + pair * HALO_PAIR) * 8)
        outside.append(jnp.where(own, 0.0, 1.0))
    group = lax.broadcasted_iota(jnp.int32, (ELEMS, LANES), 0) // GROUP
    member = (group == lax.broadcasted_iota(jnp.int32, (ELEMS, LANES), 1)).astype(jnp.float32)
    outside = jnp.concatenate(outside + outside[:2], axis=0).astype(jnp.bfloat16)
    counted[...] = jnp.dot(
        outside, member.astype(jnp.bfloat16), preferred_element_type=jnp.float32
    ).astype(jnp.int32)
    copy = pltpu.make_async_copy(counted, flags, sem)
    copy.start()
    copy.wait()

    def note(block, counts):
        counts = list(counts)
        for face in range(6):
            parity = face % 2
            active_ref[parity * LIST + counts[parity]] = face * ELEMS + block * GROUP
            counts[parity] = counts[parity] + jnp.where(flags[face, block] > 0, 1, 0)
        return tuple(counts)

    zero = jnp.zeros((), jnp.int32)
    counts = lax.fori_loop(0, ELEMS // GROUP, note, (zero, zero))
    active_ref[2 * LIST] = counts[0]
    active_ref[2 * LIST + 1] = counts[1]
    donors = donors_ref[...]
    put_words(slots_ref, 0, (donors // 8) * 24 + donors % 8)
    targets = targets_ref[...]
    put_words(slots_ref, 4, jnp.where(targets >= 0, (targets // 8) * 24 + targets % 8, STATE_ROWS))
    for copy in copies:
        copy.wait()
    state_ref[STATE_ROWS:, :] = jnp.zeros((PAD_ROWS, LANES), jnp.float32)
    for block in range(ELEMS // LANES):
        lanes = slice(block * LANES, (block + 1) * LANES)
        for c in range(3):
            turned = turn(fields_ref[c * LANES : min((c + 1) * LANES, 320), lanes])
            for r in range(16):
                state_ref[pl.ds((block * 16 + r) * 24 + c * 8, 8), :] = turned[r * 8 : r * 8 + 8]
    for tile in range(PRODUCT_TILES):
        pair, kind = tile // 5, tile % 5
        columns = []
        for c in range(3):
            lanes = slice(c * LANES, min((c + 1) * LANES, 320))
            if tile >= 15:
                rows = slice((tile - 15) * LANES, min((tile - 14) * LANES, 320))
                piece = volume_ref[rows, lanes]
            elif kind == 2:
                piece = jnp.concatenate(
                    [faces_ref[2 * pair, 256:320, lanes], faces_ref[2 * pair + 1, 256:320, lanes]], axis=0
                )
            elif kind < 2:
                piece = faces_ref[2 * pair, kind * LANES : (kind + 1) * LANES, lanes]
            else:
                piece = faces_ref[2 * pair + 1, (kind - 3) * LANES : (kind - 2) * LANES, lanes]
            columns.append(turn(piece))
        h0, l0 = split(columns[0])
        h1, l1 = split(columns[1])
        h2, l2 = split(columns[2])
        twice = jnp.concatenate([h2[0:64], h2[0:64]], axis=0)
        at = slice(tile % 2 * LANES, (tile % 2 + 1) * LANES)
        for k, part in enumerate((h0, h1, h0, h1, l0, l1, twice, l2)):
            matrix_ref[tile // 2, k * LANES : (k + 1) * LANES, at] = part.astype(jnp.bfloat16)
    zero = jnp.zeros((64, 64), jnp.float32)
    for which in range(NPAT):
        one = patterns_ref[which]
        block = jnp.concatenate(
            [jnp.concatenate([one, zero], axis=1), jnp.concatenate([zero, one], axis=1)], axis=0
        )
        high, low = split(block.T)
        at = slice(which * LANES, (which + 1) * LANES)
        for k, part in enumerate((high, high, low)):
            patterns_out[k * LANES : (k + 1) * LANES, at] = part.astype(jnp.bfloat16)


def place_kernel(
    state_ref, arrived_ref, matrix_hbm, slots_hbm, new_ref, near_ref, far_ref, third_ref, slots_ref, sems
):
    del state_ref
    slots_copy = pltpu.make_async_copy(slots_hbm, slots_ref, sems.at[0])
    slots_copy.start()
    copy = pltpu.make_async_copy(matrix_hbm.at[pl.ds(0, 3)], third_ref, sems.at[1])
    copy.start()
    slots_copy.wait()

    def body(block, carry):
        for s in range(8):
            put_row(new_ref, slots_ref[SLOTS + block * 8 + s], row(arrived_ref, block * 24 + s))
        return carry

    lax.fori_loop(0, SLOTS // 8, body, 0)
    is_odd = lax.axis_index("elem") % 2
    top = 3 * (ELEMS - HALO)
    for first, out in ((top * (1 - is_odd), near_ref), (top * is_odd, far_ref)):
        value = new_ref[pl.ds(pl.multiple_of(first, 8), 3 * HALO), :].reshape(HALO // 8, 3, 8, LANES)
        out[0:256, :] = value[:, 0].reshape(HALO, LANES)
        out[256:512, :] = value[:, 1].reshape(HALO, LANES)
        last = value[:, 2].reshape(HALO, LANES)
        out[512:640, :] = last[0:128] + pltpu.roll(last[128:256], 64, 1)
    copy.wait()


GROUP = 16


def gather_pair(table, where_ref, pair, first, count, out_ref):
    values = []
    for k in range(count):
        g = first + k
        even = tile_at(table, where_ref[2 * pair * ELEMS + g])
        odd = tile_at(table, where_ref[(2 * pair + 1) * ELEMS + g])
        value = jnp.where(even_rows(), even, odd)
        if pair > 0:
            value = value + tile_at(out_ref, g * 8)
        values.append(value)
    for k in range(count):
        out_ref[pl.ds(pl.multiple_of((first + k) * 8, 8), 8), :] = values[k]


def local_kernel(
    state_ref, third_ref, matrix_hbm, where_hbm, own_ref, gathered_ref, x, w, table0, table1, table2, where_ref, sem, sems
):
    copies = []
    for k in range(2):
        copies.append(pltpu.make_async_copy(matrix_hbm.at[pl.ds(3 * k + 3, 3)], w.at[pl.ds(3 * k, 3)], sems.at[k]))
        copies[k].start()
    copy = pltpu.make_async_copy(where_hbm, where_ref, sem)
    copy.start()
    fill_operand(x, columns_of(state_ref))
    tables = (table0, table1, table2)
    for table in tables:
        clear_tile(table, ELEMS)
    groups = ELEMS // GROUP
    for n in range(9):
        if n == 3 or n == 6:
            copies[n // 3 - 1].wait()
        factors = third_ref[n] if n < 3 else w[n - 3]
        product = jnp.dot(x[...], factors, preferred_element_type=jnp.float32)
        for half in range(2):
            tile = 2 * n + half
            block = product[:, half * LANES : (half + 1) * LANES]
            if tile < 15:
                put_tile(tables[tile // 5], 0, tile % 5, block)
            else:
                for r in range(ELEMS // 8):
                    own_ref[pl.ds(r * 24 + (tile - 15) * 8, 8), :] = block[r * 8 : r * 8 + 8]
        if n == 2:
            copy.wait()
        if n >= 3:
            part = n % 3
            for k in range(groups * part // 3, groups * (part + 1) // 3):
                gather_pair(tables[n // 3 - 1], where_ref, n // 3 - 1, k * GROUP, GROUP, gathered_ref)

    def body(k, carry):
        gather_pair(table2, where_ref, 2, k * GROUP, GROUP, gathered_ref)
        return carry

    lax.fori_loop(0, groups, body, 0)


def total(
    own_ref, gathered_ref, near_ref, far_ref, w, where_hbm, active_hbm, sums_ref, x, table, where_ref, active_ref,
    sems,
):
    del gathered_ref
    copies = [
        pltpu.make_async_copy(where_hbm, where_ref, sems.at[0]),
        pltpu.make_async_copy(active_hbm, active_ref, sems.at[1]),
    ]
    for copy in copies:
        copy.start()
    lane = lax.broadcasted_iota(jnp.int32, (128, LANES), 1)
    columns = []
    for c in range(2):
        rows = slice(c * 256, (c + 1) * 256)
        columns.append(jnp.concatenate([near_ref[rows, :], far_ref[rows, :]], axis=0))
    last = []
    for ref in (near_ref, far_ref):
        both = ref[512:640, :]
        last.append(jnp.where(lane < 64, both, 0.0))
        last.append(jnp.where(lane < 64, pltpu.roll(both, 64, 1), 0.0))
    columns.append(jnp.concatenate(last, axis=0))
    fill_operand(x, columns)
    for pair in range(3):
        clear_tile(table, pair * HALO_PAIR + 2 * HALO)
    for n in range(8):
        product = jnp.dot(x[...], w[n], preferred_element_type=jnp.float32)
        for half in range(2):
            tile = 2 * n + half
            if tile < 15:
                put_tile(table, (tile // 5) * HALO_PAIR, tile % 5, product[:, half * LANES : (half + 1) * LANES])
    for copy in copies:
        copy.wait()
    for parity in range(2):

        def body(k, carry, parity=parity):
            first = active_ref[parity * LIST + k]
            g = first & (ELEMS - 1)
            values = []
            for s in range(GROUP):
                value = tile_at(table, where_ref[first + s])
                value = jnp.where(even_rows() if parity == 0 else ~even_rows(), value, 0.0)
                values.append(tile_at(sums_ref, (g + s) * 8) + value)
            for s in range(GROUP):
                sums_ref[pl.ds(pl.multiple_of((g + s) * 8, 8), 8), :] = values[s]
            return carry

        lax.fori_loop(0, active_ref[2 * LIST + parity], body, 0)
    return [a + b for a, b in zip(columns_of(own_ref), join(sums_ref))]


def middle_kernel(
    state_ref, own_ref, gathered_ref, near_ref, far_ref, w, where_hbm, active_hbm, jacobian_ref,
    slots_hbm, choose_ref, patterns_ref,
    new_ref, out_ref, sums_ref,
    x, table, where_ref, active_ref, sems, picked, operand, slots_ref, sem,
):
    copy = pltpu.make_async_copy(slots_hbm, slots_ref, sem)
    copy.start()
    sums = total(
        own_ref, gathered_ref, near_ref, far_ref, w, where_hbm, active_hbm, sums_ref, x, table, where_ref,
        active_ref, sems,
    )
    factor = 0.25 * down(jacobian_ref, ELEMS)
    put_columns(new_ref, [w + factor * a for w, a in zip(columns_of(state_ref), sums)])
    new_ref[STATE_ROWS:, :] = jnp.zeros((PAD_ROWS, LANES), jnp.float32)
    copy.wait()
    send_blocks(new_ref, slots_ref, choose_ref, patterns_ref, out_ref, picked, operand)


def last_kernel(
    first_ref, state_ref, own_ref, gathered_ref, near_ref, far_ref, w, where_hbm, active_hbm,
    jacobian_ref,
    out_hbm, sums_ref,
    x, table, where_ref, active_ref, sems, out_ref, out_sems,
):
    sums = total(
        own_ref, gathered_ref, near_ref, far_ref, w, where_hbm, active_hbm, sums_ref, x, table, where_ref,
        active_ref, sems,
    )
    factor = 0.25 * down(jacobian_ref, ELEMS)
    copies = []
    for c, (f, w, a) in enumerate(zip(columns_of(first_ref), columns_of(state_ref), sums)):
        result = 0.5 * f + 0.5 * (w + factor * a)
        rows = min(LANES, 320 - c * LANES)
        at = pl.ds(c * LANES, rows)
        out_ref[at, :] = result.T[0:rows]
        copies.append(pltpu.make_async_copy(out_ref.at[at], out_hbm.at[at], out_sems.at[c]))
        copies[c].start()
    for copy in copies:
        copy.wait()


def estimate(flops, size):
    return pl.CostEstimate(flops=flops, bytes_accessed=size, transcendentals=0)


STATE = (STATE_ROWS + PAD_ROWS, LANES)
MESSAGE = (MESSAGE_ROWS, LANES)
RIM = (640, LANES)
GATHERED = (ELEMS * 8, LANES)


def near(shape, dtype=jnp.float32):
    return pltpu.VMEM(shape, dtype)


def held(value):
    return pltpu.with_memory_space_constraint(value, pltpu.VMEM)


def call(kernel, name, outs, specs, scratch, cost, *args, aliases=None, out_specs=None):
    args = [held(a) if spec is VMEM_HELD else a for a, spec in zip(args, specs)]
    return pl.pallas_call(
        kernel,
        out_shape=outs,
        in_specs=[VMEM if spec is VMEM_HELD else spec for spec in specs],
        out_specs=out_specs or (tuple(VMEM for _ in outs) if isinstance(outs, tuple) else VMEM),
        input_output_aliases=aliases or {},
        scratch_shapes=scratch,
        compiler_params=pltpu.CompilerParams(vmem_limit_bytes=VMEM_LIMIT),
        cost_estimate=cost,
        name=name,
    )(*args)


VMEM_HELD = object()
H = VMEM_HELD


def near_scratch(*shape, dtype=jnp.float32):
    return pltpu.VMEM(shape, dtype)


LOCAL_SCRATCH = (
    [near_scratch(ELEMS, 1024, dtype=jnp.bfloat16), near_scratch(6, 1024, 256, dtype=jnp.bfloat16)]
    + [near_scratch(LOCAL_PAIR * 8, LANES)] * 3
    + [pltpu.SMEM((6 * ELEMS,), jnp.int32), pltpu.SemaphoreType.DMA(()), pltpu.SemaphoreType.DMA((2,))]
)
HALO_SCRATCH = [
    near_scratch(2 * HALO, 1024, dtype=jnp.bfloat16), near_scratch(3 * HALO_PAIR * 8, LANES),
    pltpu.SMEM((6 * ELEMS,), jnp.int32), pltpu.SMEM((1024,), jnp.int32), pltpu.SemaphoreType.DMA((2,)),
]
SEND_SCRATCH = [
    pltpu.VMEM((MESSAGE_ROWS + 8, LANES), jnp.float32),
    pltpu.VMEM((MESSAGE_ROWS, 3 * LANES), jnp.bfloat16),
    pltpu.SMEM((1024,), jnp.int32), pltpu.SemaphoreType.DMA(()),
]


def words(rows):
    return jax.ShapeDtypeStruct((rows, LANES), jnp.int32)


def swap(message):
    return lax.ppermute(message, "sec", [(0, 1), (1, 0)])


def spread(crossed):
    blocks = crossed.reshape(64, MESSAGE_ROWS // 64, LANES)
    return lax.all_to_all(blocks, "elem", 0, 0, tiled=True).reshape(MESSAGE_ROWS, LANES)


def rims(near_rim, far_rim):
    count = lax.axis_size("elem")

    def swaps(first):
        pairs = [(i, i + 1) for i in range(first, count - 1, 2)]
        return pairs + [(b, a) for a, b in pairs]

    return lax.ppermute(near_rim, "elem", swaps(0)), lax.ppermute(far_rim, "elem", swaps(1))


def local(
    fields,
    jacobian,
    face_links,
    volume_matrix,
    face_matrices,
    patterns,
    donor_index,
    pattern_index,
    receivers,
):
    message = call(
        start_kernel, "start", near(MESSAGE), [HBM] * 4,
        [
            pltpu.VMEM((640, ELEMS), jnp.bfloat16), pltpu.VMEM((ELEMS, SLOTS), jnp.bfloat16),
            pltpu.VMEM((320, ELEMS), jnp.float32), pltpu.VMEM((1, SLOTS), jnp.int32),
            pltpu.VMEM((1, SLOTS), jnp.int32), pltpu.VMEM((NPAT, 64, 64), jnp.float32),
            pltpu.SemaphoreType.DMA((4,)),
        ],
        estimate(10**9, 2 * 10**6),
        *[pltpu.with_memory_space_constraint(v, pltpu.HBM) for v in (fields[0], donor_index, pattern_index, patterns)],
    )
    crossed = swap(message)
    arrived = spread(crossed)
    far = [pltpu.with_memory_space_constraint(v, pltpu.HBM) for v in (fields[0], volume_matrix[0], face_matrices[0])]
    state, matrix, pattern_blocks, local_rows, rim_rows, slots, active = call(
        prepare_kernel, "prepare",
        (
            near(STATE), near((9, 1024, 256), jnp.bfloat16), near((3 * LANES, NPAT * LANES), jnp.bfloat16),
            words(48), words(48), words(8), jax.ShapeDtypeStruct((1024,), jnp.int32),
        ),
        [HBM, VMEM, HBM, HBM] + [VMEM] * 3 + [ANY],
        [
            pltpu.VMEM((8, LANES), jnp.int32), pltpu.SMEM((8, LANES), jnp.int32),
            near_scratch(320, ELEMS), near_scratch(320, 320), near_scratch(6, 320, 320),
            pltpu.SemaphoreType.DMA(()), pltpu.SemaphoreType.DMA((3,)),
        ],
        estimate(2 * 10**10, 40 * 10**6),
        far[0], face_links[0], far[1], far[2], patterns, donor_index, receivers, crossed,
        out_specs=(VMEM,) * 6 + (SMEM,),
    )
    local_rows, rim_rows, slots = [v.reshape(-1) for v in (local_rows, rim_rows, slots)]

    def settle(values, arrived):
        return call(
            place_kernel, "place", (near(STATE), near(RIM), near(RIM), near((3, 1024, 256), jnp.bfloat16)),
            [H, H, HBM, ANY], [pltpu.SMEM((1024,), jnp.int32), pltpu.SemaphoreType.DMA((2,))],
            estimate(10**6, 4 * 10**6), values, arrived, pltpu.with_memory_space_constraint(matrix, pltpu.HBM), slots,
            aliases={0: 0},
        )

    def local_sum(values, third):
        return call(
            local_kernel, "local_sum", (near((STATE_ROWS, LANES)), near(GATHERED)), [H, H, HBM, ANY],
            LOCAL_SCRATCH, estimate(10**10, 30 * 10**6),
            values, third, pltpu.with_memory_space_constraint(matrix, pltpu.HBM), local_rows,
        )

    first, near_rim, far_rim, third = settle(state, arrived)
    near_got, far_got = rims(near_rim, far_rim)
    own, gathered = local_sum(first, third)
    middle, message, _ = call(
        middle_kernel, "middle_step", (near(STATE), near(MESSAGE), near(GATHERED)),
        [H] * 6 + [ANY, ANY, VMEM, ANY, VMEM, H], HALO_SCRATCH + SEND_SCRATCH, estimate(6 * 10**9, 10**7),
        first, own, gathered, near_got, far_got, matrix, rim_rows, active, jacobian, slots, pattern_index, pattern_blocks,
        aliases={2: 2},
    )
    arrived = spread(swap(message))
    second, near_rim, far_rim, third = settle(middle, arrived)
    near_got, far_got = rims(near_rim, far_rim)
    own, gathered = local_sum(second, third)
    advanced, _ = call(
        last_kernel, "last_step", (jax.ShapeDtypeStruct((320, ELEMS), jnp.float32), near(GATHERED)),
        [H] * 7 + [ANY, ANY, VMEM], HALO_SCRATCH + [near_scratch(320, ELEMS), pltpu.SemaphoreType.DMA((3,))], estimate(6 * 10**9, 10**7),
        first, second, own, gathered, near_got, far_got, matrix, rim_rows, active, jacobian,
        aliases={3: 1}, out_specs=(HBM, VMEM),
    )
    return advanced[None]


def solution(mesh):
    return jax.shard_map(
        local,
        mesh=mesh,
        in_specs=(
            P("sec", None, "elem"),
            P("sec", "elem"),
            P("sec", None, "elem"),
            P("sec", None, None),
            P("sec", None, None, None),
            P(),
            P("sec", "elem"),
            P("sec", "elem"),
            P("sec", "elem"),
        ),
        out_specs=P("sec", None, "elem"),
        check_vma=False,
    )
```

```python
import jax
import jax.numpy as jnp
from jax import lax
from jax.experimental import pallas as pl
from jax.experimental.pallas import tpu as pltpu
from jax.sharding import PartitionSpec as P

NPAT = 4
HALO = 256
ELEMS = 1024
SLOTS = 512
LANES = 128
STATE_ROWS = ELEMS * 3
PAD_ROWS = 24
MESSAGE_ROWS = SLOTS * 3
LOCAL_PAIR = ELEMS + 8
HALO_PAIR = 2 * HALO + 8
PRODUCT_TILES = 18
LIST = 400
VMEM_LIMIT = 28 * 1024 * 1024

VMEM = pl.BlockSpec(memory_space=pltpu.VMEM)
SMEM = pl.BlockSpec(memory_space=pltpu.SMEM)
ANY = pl.BlockSpec(memory_space=pl.ANY)
HBM = pl.BlockSpec(memory_space=pltpu.HBM)


def row(ref, start):
    return ref[pl.ds(start, 3, stride=8), :]


def put_row(ref, start, value):
    ref[pl.ds(start, 3, stride=8), :] = value


def tiles_of(value, count):
    return value.reshape(count // 8, 3, 8, LANES)


def split(value):
    high = value.astype(jnp.bfloat16).astype(jnp.float32)
    return high, value - high


def fill_operand(x_ref, columns):
    h0, l0 = split(columns[0])
    h1, l1 = split(columns[1])
    h2, l2 = split(columns[2])
    both = h2 + pltpu.roll(l2, 64, 1)
    for k, part in enumerate((h0, h1, l0, l1, h0, h1, both, h2)):
        x_ref[:, k * LANES : (k + 1) * LANES] = part.astype(jnp.bfloat16)


def put_tile(table, element, tile, block):
    for r in range(block.shape[0] // 8):
        start = pl.multiple_of((element + r * 8) * 8, 64)
        table[pl.ds(start + tile, 8, stride=8), :] = block[r * 8 : r * 8 + 8]


def even_rows():
    sub = lax.broadcasted_iota(jnp.int32, (8, LANES), 0)
    lane = lax.broadcasted_iota(jnp.int32, (8, LANES), 1)
    return (sub < 2) | ((sub == 2) & (lane < 64))


def tile_at(table, place):
    return table[pl.ds(pl.multiple_of(place, 8), 8), :]


def clear_tile(table, element):
    table[pl.ds(element * 8, 8), :] = jnp.zeros((8, LANES), jnp.float32)


def join(ref):
    part = [ref[pl.ds(c, ELEMS, stride=8), :] for c in range(5)]
    lane = lax.broadcasted_iota(jnp.int32, (ELEMS, LANES), 1)
    last = jnp.where(lane < 64, part[2] + pltpu.roll(part[2], 64, 1), 0.0)
    return part[0] + part[3], part[1] + part[4], last


def columns_of(ref):
    value = tiles_of(ref[0:STATE_ROWS, :], ELEMS)
    return [value[:, c].reshape(ELEMS, LANES) for c in range(3)]


def put_columns(ref, columns):
    stacked = jnp.stack([c.reshape(ELEMS // 8, 8, LANES) for c in columns], axis=1)
    ref[0:STATE_ROWS, :] = stacked.reshape(STATE_ROWS, LANES)


def send_blocks(state_ref, donors_ref, choose_ref, patterns_ref, out_ref, picked, operand):
    def body(block, carry):
        for s in range(8):
            put_row(picked, block * 24 + s, row(state_ref, donors_ref[block * 8 + s]))
        return carry

    lax.fori_loop(0, SLOTS // 8, body, 0)
    high, low = split(picked[0:MESSAGE_ROWS])
    for k, part in enumerate((high, low, high)):
        operand[:, k * LANES : (k + 1) * LANES] = part.astype(jnp.bfloat16)
    mapped = jnp.dot(operand[...], patterns_ref[...], preferred_element_type=jnp.float32)
    choose = down(choose_ref, SLOTS).reshape(SLOTS // 8, 1, 8, LANES)
    result = tiles_of(mapped[:, :LANES], SLOTS)
    for which in range(1, NPAT):
        other = tiles_of(mapped[:, which * LANES : (which + 1) * LANES], SLOTS)
        result = jnp.where(choose == which, other, result)
    out_ref[...] = result.reshape(MESSAGE_ROWS, LANES)


def start_kernel(
    fields_hbm, donors_hbm, choose_hbm, patterns_hbm, out_ref,
    both, chosen, fields_ref, donors_ref, choose_ref, patterns_ref, sems,
):
    pairs = (
        (donors_hbm, donors_ref), (choose_hbm, choose_ref), (patterns_hbm, patterns_ref), (fields_hbm, fields_ref)
    )
    copies = [pltpu.make_async_copy(a, b, sems.at[k]) for k, (a, b) in enumerate(pairs)]
    for copy in copies[::-1]:
        copy.start()
    copies[0].wait()
    element = lax.broadcasted_iota(jnp.int32, (ELEMS, SLOTS), 0)
    chosen[...] = (element == donors_ref[...]).astype(jnp.float32).astype(jnp.bfloat16)
    for copy in copies[1:]:
        copy.wait()
    high, low = split(fields_ref[...])
    both[0:320, :] = high.astype(jnp.bfloat16)
    both[320:640, :] = low.astype(jnp.bfloat16)
    picked = jnp.dot(both[...], chosen[...], preferred_element_type=jnp.float32)
    high = picked[0:320].astype(jnp.bfloat16)
    low = picked[320:640].astype(jnp.bfloat16)
    patterns_high, patterns_low = split(patterns_ref[...].reshape(NPAT * 64, 64))
    weights = jnp.concatenate([patterns_high, patterns_high, patterns_low], axis=1).astype(jnp.bfloat16)
    which = choose_ref[...]
    results = []
    for v in range(5):
        rows = slice(v * 64, (v + 1) * 64)
        operand = jnp.concatenate([high[rows], low[rows], high[rows]], axis=0)
        mapped = jnp.dot(weights, operand, preferred_element_type=jnp.float32)
        result = mapped[0:64]
        for p in range(1, NPAT):
            result = jnp.where(which == p, mapped[p * 64 : (p + 1) * 64], result)
        results.append(result)
    results.append(jnp.zeros((64, SLOTS), jnp.float32))
    for c in range(3):
        tall = jnp.concatenate([results[2 * c], results[2 * c + 1]], axis=0)
        for block in range(SLOTS // LANES):
            turned = tall[:, block * LANES : (block + 1) * LANES].T
            for r in range(16):
                out_ref[pl.ds((block * 16 + r) * 24 + c * 8, 8), :] = turned[r * 8 : r * 8 + 8]


def down(ref, count):
    columns = []
    for block in range(count // LANES):
        value = ref[:, block * LANES : (block + 1) * LANES].astype(jnp.float32)
        columns.append(jnp.broadcast_to(value, (LANES, LANES)).T)
    return jnp.concatenate(columns, axis=0)


def turn(piece):
    missing = LANES - piece.shape[0], LANES - piece.shape[1]
    if missing[1]:
        piece = jnp.concatenate([piece, jnp.zeros((piece.shape[0], missing[1]), jnp.float32)], axis=1)
    if missing[0]:
        piece = jnp.concatenate([piece, jnp.zeros((missing[0], LANES), jnp.float32)], axis=0)
    return piece.T


def put_words(out_ref, first, value):
    for k in range(value.shape[1] // LANES):
        out_ref[first + k : first + k + 1, :] = value[:, k * LANES : (k + 1) * LANES]


def prepare_kernel(
    fields_hbm, links_ref, volume_hbm, faces_hbm, patterns_ref, donors_ref, targets_ref, after_ref,
    state_ref, matrix_ref, patterns_out,
    local_ref, rim_ref, slots_ref, active_ref,
    counted, flags, fields_ref, volume_ref, faces_ref, sem, sems,
):
    del after_ref
    pairs = ((fields_hbm, fields_ref), (volume_hbm, volume_ref), (faces_hbm, faces_ref))
    copies = [pltpu.make_async_copy(a, b, sems.at[k]) for k, (a, b) in enumerate(pairs)]
    for copy in copies:
        copy.start()
    outside = []
    is_odd = lax.axis_index("elem") % 2
    for face in range(6):
        links = links_ref[face : face + 1, :]
        own = (links >= HALO) & (links < HALO + ELEMS)
        pair = face // 2
        put_words(local_ref, face * 8, jnp.where(own, links - HALO, ELEMS) * 8)
        rim = jnp.where(links < HALO, links + HALO * (1 - is_odd), links - (HALO + ELEMS) + HALO * is_odd)
        put_words(rim_ref, face * 8, (jnp.where(own, 2 * HALO, rim) + pair * HALO_PAIR) * 8)
        outside.append(jnp.where(own, 0.0, 1.0))
    group = lax.broadcasted_iota(jnp.int32, (ELEMS, LANES), 0) // GROUP
    member = (group == lax.broadcasted_iota(jnp.int32, (ELEMS, LANES), 1)).astype(jnp.float32)
    outside = jnp.concatenate(outside + outside[:2], axis=0).astype(jnp.bfloat16)
    counted[...] = jnp.dot(
        outside, member.astype(jnp.bfloat16), preferred_element_type=jnp.float32
    ).astype(jnp.int32)
    copy = pltpu.make_async_copy(counted, flags, sem)
    copy.start()
    copy.wait()

    def note(block, counts):
        counts = list(counts)
        for face in range(6):
            parity = face % 2
            active_ref[parity * LIST + counts[parity]] = face * ELEMS + block * GROUP
            counts[parity] = counts[parity] + jnp.where(flags[face, block] > 0, 1, 0)
        return tuple(counts)

    zero = jnp.zeros((), jnp.int32)
    counts = lax.fori_loop(0, ELEMS // GROUP, note, (zero, zero))
    active_ref[2 * LIST] = counts[0]
    active_ref[2 * LIST + 1] = counts[1]
    donors = donors_ref[...]
    put_words(slots_ref, 0, (donors // 8) * 24 + donors % 8)
    targets = targets_ref[...]
    put_words(slots_ref, 4, jnp.where(targets >= 0, (targets // 8) * 24 + targets % 8, STATE_ROWS))
    for copy in copies:
        copy.wait()
    state_ref[STATE_ROWS:, :] = jnp.zeros((PAD_ROWS, LANES), jnp.float32)
    for block in range(ELEMS // LANES):
        lanes = slice(block * LANES, (block + 1) * LANES)
        for c in range(3):
            turned = turn(fields_ref[c * LANES : min((c + 1) * LANES, 320), lanes])
            for r in range(16):
                state_ref[pl.ds((block * 16 + r) * 24 + c * 8, 8), :] = turned[r * 8 : r * 8 + 8]
    for tile in range(PRODUCT_TILES):
        pair, kind = tile // 5, tile % 5
        columns = []
        for c in range(3):
            lanes = slice(c * LANES, min((c + 1) * LANES, 320))
            if tile >= 15:
                rows = slice((tile - 15) * LANES, min((tile - 14) * LANES, 320))
                piece = volume_ref[rows, lanes]
            elif kind == 2:
                piece = jnp.concatenate(
                    [faces_ref[2 * pair, 256:320, lanes], faces_ref[2 * pair + 1, 256:320, lanes]], axis=0
                )
            elif kind < 2:
                piece = faces_ref[2 * pair, kind * LANES : (kind + 1) * LANES, lanes]
            else:
                piece = faces_ref[2 * pair + 1, (kind - 3) * LANES : (kind - 2) * LANES, lanes]
            columns.append(turn(piece))
        h0, l0 = split(columns[0])
        h1, l1 = split(columns[1])
        h2, l2 = split(columns[2])
        twice = jnp.concatenate([h2[0:64], h2[0:64]], axis=0)
        at = slice(tile % 2 * LANES, (tile % 2 + 1) * LANES)
        for k, part in enumerate((h0, h1, h0, h1, l0, l1, twice, l2)):
            matrix_ref[tile // 2, k * LANES : (k + 1) * LANES, at] = part.astype(jnp.bfloat16)
    zero = jnp.zeros((64, 64), jnp.float32)
    for which in range(NPAT):
        one = patterns_ref[which]
        block = jnp.concatenate(
            [jnp.concatenate([one, zero], axis=1), jnp.concatenate([zero, one], axis=1)], axis=0
        )
        high, low = split(block.T)
        at = slice(which * LANES, (which + 1) * LANES)
        for k, part in enumerate((high, high, low)):
            patterns_out[k * LANES : (k + 1) * LANES, at] = part.astype(jnp.bfloat16)


def place_kernel(
    state_ref, arrived_ref, matrix_hbm, slots_hbm, new_ref, near_ref, far_ref, third_ref, slots_ref, sems
):
    del state_ref
    slots_copy = pltpu.make_async_copy(slots_hbm, slots_ref, sems.at[0])
    slots_copy.start()
    copy = pltpu.make_async_copy(matrix_hbm.at[pl.ds(0, 3)], third_ref, sems.at[1])
    copy.start()
    slots_copy.wait()

    def body(block, carry):
        for s in range(8):
            put_row(new_ref, slots_ref[SLOTS + block * 8 + s], row(arrived_ref, block * 24 + s))
        return carry

    lax.fori_loop(0, SLOTS // 8, body, 0)
    is_odd = lax.axis_index("elem") % 2
    top = 3 * (ELEMS - HALO)
    for first, out in ((top * (1 - is_odd), near_ref), (top * is_odd, far_ref)):
        value = new_ref[pl.ds(pl.multiple_of(first, 8), 3 * HALO), :].reshape(HALO // 8, 3, 8, LANES)
        out[0:256, :] = value[:, 0].reshape(HALO, LANES)
        out[256:512, :] = value[:, 1].reshape(HALO, LANES)
        last = value[:, 2].reshape(HALO, LANES)
        out[512:640, :] = last[0:128] + pltpu.roll(last[128:256], 64, 1)
    copy.wait()


GROUP = 16


def gather_pair(table, where_ref, pair, first, count, out_ref):
    values = []
    for k in range(count):
        g = first + k
        even = tile_at(table, where_ref[2 * pair * ELEMS + g])
        odd = tile_at(table, where_ref[(2 * pair + 1) * ELEMS + g])
        value = jnp.where(even_rows(), even, odd)
        if pair > 0:
            value = value + tile_at(out_ref, g * 8)
        values.append(value)
    for k in range(count):
        out_ref[pl.ds(pl.multiple_of((first + k) * 8, 8), 8), :] = values[k]


def local_kernel(
    state_ref, third_ref, matrix_hbm, where_hbm, own_ref, gathered_ref, x, w, table0, table1, table2, where_ref, sem, sems
):
    copies = []
    for k in range(2):
        copies.append(pltpu.make_async_copy(matrix_hbm.at[pl.ds(3 * k + 3, 3)], w.at[pl.ds(3 * k, 3)], sems.at[k]))
        copies[k].start()
    copy = pltpu.make_async_copy(where_hbm, where_ref, sem)
    copy.start()
    fill_operand(x, columns_of(state_ref))
    tables = (table0, table1, table2)
    for table in tables:
        clear_tile(table, ELEMS)
    groups = ELEMS // GROUP
    for n in range(9):
        if n == 3 or n == 6:
            copies[n // 3 - 1].wait()
        factors = third_ref[n] if n < 3 else w[n - 3]
        product = jnp.dot(x[...], factors, preferred_element_type=jnp.float32)
        for half in range(2):
            tile = 2 * n + half
            block = product[:, half * LANES : (half + 1) * LANES]
            if tile < 15:
                put_tile(tables[tile // 5], 0, tile % 5, block)
            else:
                for r in range(ELEMS // 8):
                    own_ref[pl.ds(r * 24 + (tile - 15) * 8, 8), :] = block[r * 8 : r * 8 + 8]
        if n == 2:
            copy.wait()
        if n >= 3:
            part = n % 3
            for k in range(groups * part // 3, groups * (part + 1) // 3):
                gather_pair(tables[n // 3 - 1], where_ref, n // 3 - 1, k * GROUP, GROUP, gathered_ref)

    def body(k, carry):
        gather_pair(table2, where_ref, 2, k * 2 * GROUP, 2 * GROUP, gathered_ref)
        return carry

    lax.fori_loop(0, groups // 2, body, 0)


def total(
    own_ref, gathered_ref, near_ref, far_ref, w, where_hbm, active_hbm, sums_ref, x, table, where_ref, active_ref,
    sems,
):
    del gathered_ref
    copies = [
        pltpu.make_async_copy(where_hbm, where_ref, sems.at[0]),
        pltpu.make_async_copy(active_hbm, active_ref, sems.at[1]),
    ]
    for copy in copies:
        copy.start()
    lane = lax.broadcasted_iota(jnp.int32, (128, LANES), 1)
    columns = []
    for c in range(2):
        rows = slice(c * 256, (c + 1) * 256)
        columns.append(jnp.concatenate([near_ref[rows, :], far_ref[rows, :]], axis=0))
    last = []
    for ref in (near_ref, far_ref):
        both = ref[512:640, :]
        last.append(jnp.where(lane < 64, both, 0.0))
        last.append(jnp.where(lane < 64, pltpu.roll(both, 64, 1), 0.0))
    columns.append(jnp.concatenate(last, axis=0))
    fill_operand(x, columns)
    for pair in range(3):
        clear_tile(table, pair * HALO_PAIR + 2 * HALO)
    for n in range(8):
        halves = 2 if n < 7 else 1
        product = jnp.dot(x[...], w[n, :, 0 : halves * LANES], preferred_element_type=jnp.float32)
        for half in range(halves):
            tile = 2 * n + half
            put_tile(table, (tile // 5) * HALO_PAIR, tile % 5, product[:, half * LANES : (half + 1) * LANES])
    for copy in copies:
        copy.wait()
    for parity in range(2):

        def body(k, carry, parity=parity):
            first = active_ref[parity * LIST + k]
            g = first & (ELEMS - 1)
            values = []
            for s in range(GROUP):
                value = tile_at(table, where_ref[first + s])
                value = jnp.where(even_rows() if parity == 0 else ~even_rows(), value, 0.0)
                values.append(tile_at(sums_ref, (g + s) * 8) + value)
            for s in range(GROUP):
                sums_ref[pl.ds(pl.multiple_of((g + s) * 8, 8), 8), :] = values[s]
            return carry

        lax.fori_loop(0, active_ref[2 * LIST + parity], body, 0)
    return [a + b for a, b in zip(columns_of(own_ref), join(sums_ref))]


def middle_kernel(
    state_ref, own_ref, gathered_ref, near_ref, far_ref, w, where_hbm, active_hbm, jacobian_ref,
    slots_hbm, choose_ref, patterns_ref,
    new_ref, out_ref, sums_ref,
    x, table, where_ref, active_ref, sems, picked, operand, slots_ref, sem,
):
    copy = pltpu.make_async_copy(slots_hbm, slots_ref, sem)
    copy.start()
    sums = total(
        own_ref, gathered_ref, near_ref, far_ref, w, where_hbm, active_hbm, sums_ref, x, table, where_ref,
        active_ref, sems,
    )
    factor = 0.25 * down(jacobian_ref, ELEMS)
    put_columns(new_ref, [w + factor * a for w, a in zip(columns_of(state_ref), sums)])
    new_ref[STATE_ROWS:, :] = jnp.zeros((PAD_ROWS, LANES), jnp.float32)
    copy.wait()
    send_blocks(new_ref, slots_ref, choose_ref, patterns_ref, out_ref, picked, operand)


def last_kernel(
    first_ref, state_ref, own_ref, gathered_ref, near_ref, far_ref, w, where_hbm, active_hbm,
    jacobian_ref,
    out_hbm, sums_ref,
    x, table, where_ref, active_ref, sems, out_ref, out_sems,
):
    sums = total(
        own_ref, gathered_ref, near_ref, far_ref, w, where_hbm, active_hbm, sums_ref, x, table, where_ref,
        active_ref, sems,
    )
    factor = 0.25 * down(jacobian_ref, ELEMS)
    copies = []
    for c, (f, w, a) in enumerate(zip(columns_of(first_ref), columns_of(state_ref), sums)):
        result = 0.5 * f + 0.5 * (w + factor * a)
        rows = min(LANES, 320 - c * LANES)
        at = pl.ds(c * LANES, rows)
        out_ref[at, :] = result.T[0:rows]
        copies.append(pltpu.make_async_copy(out_ref.at[at], out_hbm.at[at], out_sems.at[c]))
        copies[c].start()
    for copy in copies:
        copy.wait()


def estimate(flops, size):
    return pl.CostEstimate(flops=flops, bytes_accessed=size, transcendentals=0)


STATE = (STATE_ROWS + PAD_ROWS, LANES)
MESSAGE = (MESSAGE_ROWS, LANES)
RIM = (640, LANES)
GATHERED = (ELEMS * 8, LANES)


def near(shape, dtype=jnp.float32):
    return pltpu.VMEM(shape, dtype)


def held(value):
    return pltpu.with_memory_space_constraint(value, pltpu.VMEM)


def call(kernel, name, outs, specs, scratch, cost, *args, aliases=None, out_specs=None):
    args = [held(a) if spec is VMEM_HELD else a for a, spec in zip(args, specs)]
    return pl.pallas_call(
        kernel,
        out_shape=outs,
        in_specs=[VMEM if spec is VMEM_HELD else spec for spec in specs],
        out_specs=out_specs or (tuple(VMEM for _ in outs) if isinstance(outs, tuple) else VMEM),
        input_output_aliases=aliases or {},
        scratch_shapes=scratch,
        compiler_params=pltpu.CompilerParams(vmem_limit_bytes=VMEM_LIMIT),
        cost_estimate=cost,
        name=name,
    )(*args)


VMEM_HELD = object()
H = VMEM_HELD


def near_scratch(*shape, dtype=jnp.float32):
    return pltpu.VMEM(shape, dtype)


LOCAL_SCRATCH = (
    [near_scratch(ELEMS, 1024, dtype=jnp.bfloat16), near_scratch(6, 1024, 256, dtype=jnp.bfloat16)]
    + [near_scratch(LOCAL_PAIR * 8, LANES)] * 3
    + [pltpu.SMEM((6 * ELEMS,), jnp.int32), pltpu.SemaphoreType.DMA(()), pltpu.SemaphoreType.DMA((2,))]
)
HALO_SCRATCH = [
    near_scratch(2 * HALO, 1024, dtype=jnp.bfloat16), near_scratch(3 * HALO_PAIR * 8, LANES),
    pltpu.SMEM((6 * ELEMS,), jnp.int32), pltpu.SMEM((1024,), jnp.int32), pltpu.SemaphoreType.DMA((2,)),
]
SEND_SCRATCH = [
    pltpu.VMEM((MESSAGE_ROWS + 8, LANES), jnp.float32),
    pltpu.VMEM((MESSAGE_ROWS, 3 * LANES), jnp.bfloat16),
    pltpu.SMEM((1024,), jnp.int32), pltpu.SemaphoreType.DMA(()),
]


def words(rows):
    return jax.ShapeDtypeStruct((rows, LANES), jnp.int32)


def swap(message):
    return lax.ppermute(message, "sec", [(0, 1), (1, 0)])


def spread(crossed):
    blocks = crossed.reshape(64, MESSAGE_ROWS // 64, LANES)
    return lax.all_to_all(blocks, "elem", 0, 0, tiled=True).reshape(MESSAGE_ROWS, LANES)


def rims(near_rim, far_rim):
    count = lax.axis_size("elem")

    def swaps(first):
        pairs = [(i, i + 1) for i in range(first, count - 1, 2)]
        return pairs + [(b, a) for a, b in pairs]

    return lax.ppermute(near_rim, "elem", swaps(0)), lax.ppermute(far_rim, "elem", swaps(1))


def local(
    fields,
    jacobian,
    face_links,
    volume_matrix,
    face_matrices,
    patterns,
    donor_index,
    pattern_index,
    receivers,
):
    message = call(
        start_kernel, "start", near(MESSAGE), [HBM] * 4,
        [
            pltpu.VMEM((640, ELEMS), jnp.bfloat16), pltpu.VMEM((ELEMS, SLOTS), jnp.bfloat16),
            pltpu.VMEM((320, ELEMS), jnp.float32), pltpu.VMEM((1, SLOTS), jnp.int32),
            pltpu.VMEM((1, SLOTS), jnp.int32), pltpu.VMEM((NPAT, 64, 64), jnp.float32),
            pltpu.SemaphoreType.DMA((4,)),
        ],
        estimate(10**9, 2 * 10**6),
        *[pltpu.with_memory_space_constraint(v, pltpu.HBM) for v in (fields[0], donor_index, pattern_index, patterns)],
    )
    crossed = swap(message)
    arrived = spread(crossed)
    far = [pltpu.with_memory_space_constraint(v, pltpu.HBM) for v in (fields[0], volume_matrix[0], face_matrices[0])]
    state, matrix, pattern_blocks, local_rows, rim_rows, slots, active = call(
        prepare_kernel, "prepare",
        (
            near(STATE), near((9, 1024, 256), jnp.bfloat16), near((3 * LANES, NPAT * LANES), jnp.bfloat16),
            words(48), words(48), words(8), jax.ShapeDtypeStruct((1024,), jnp.int32),
        ),
        [HBM, VMEM, HBM, HBM] + [VMEM] * 3 + [ANY],
        [
            pltpu.VMEM((8, LANES), jnp.int32), pltpu.SMEM((8, LANES), jnp.int32),
            near_scratch(320, ELEMS), near_scratch(320, 320), near_scratch(6, 320, 320),
            pltpu.SemaphoreType.DMA(()), pltpu.SemaphoreType.DMA((3,)),
        ],
        estimate(2 * 10**10, 40 * 10**6),
        far[0], face_links[0], far[1], far[2], patterns, donor_index, receivers, crossed,
        out_specs=(VMEM,) * 6 + (SMEM,),
    )
    local_rows, rim_rows, slots = [v.reshape(-1) for v in (local_rows, rim_rows, slots)]

    def settle(values, arrived):
        return call(
            place_kernel, "place", (near(STATE), near(RIM), near(RIM), near((3, 1024, 256), jnp.bfloat16)),
            [H, H, HBM, ANY], [pltpu.SMEM((1024,), jnp.int32), pltpu.SemaphoreType.DMA((2,))],
            estimate(10**6, 4 * 10**6), values, arrived, pltpu.with_memory_space_constraint(matrix, pltpu.HBM), slots,
            aliases={0: 0},
        )

    def local_sum(values, third):
        return call(
            local_kernel, "local_sum", (near((STATE_ROWS, LANES)), near(GATHERED)), [H, H, HBM, ANY],
            LOCAL_SCRATCH, estimate(10**10, 30 * 10**6),
            values, third, pltpu.with_memory_space_constraint(matrix, pltpu.HBM), local_rows,
        )

    first, near_rim, far_rim, third = settle(state, arrived)
    near_got, far_got = rims(near_rim, far_rim)
    own, gathered = local_sum(first, third)
    middle, message, _ = call(
        middle_kernel, "middle_step", (near(STATE), near(MESSAGE), near(GATHERED)),
        [H] * 6 + [ANY, ANY, VMEM, ANY, VMEM, H], HALO_SCRATCH + SEND_SCRATCH, estimate(6 * 10**9, 10**7),
        first, own, gathered, near_got, far_got, matrix, rim_rows, active, jacobian, slots, pattern_index, pattern_blocks,
        aliases={2: 2},
    )
    arrived = spread(swap(message))
    second, near_rim, far_rim, third = settle(middle, arrived)
    near_got, far_got = rims(near_rim, far_rim)
    own, gathered = local_sum(second, third)
    advanced, _ = call(
        last_kernel, "last_step", (jax.ShapeDtypeStruct((320, ELEMS), jnp.float32), near(GATHERED)),
        [H] * 7 + [ANY, ANY, VMEM], HALO_SCRATCH + [near_scratch(320, ELEMS), pltpu.SemaphoreType.DMA((3,))], estimate(6 * 10**9, 10**7),
        first, second, own, gathered, near_got, far_got, matrix, rim_rows, active, jacobian,
        aliases={3: 1}, out_specs=(HBM, VMEM),
    )
    return advanced[None]


def solution(mesh):
    return jax.shard_map(
        local,
        mesh=mesh,
        in_specs=(
            P("sec", None, "elem"),
            P("sec", "elem"),
            P("sec", None, "elem"),
            P("sec", None, None),
            P("sec", None, None, None),
            P(),
            P("sec", "elem"),
            P("sec", "elem"),
            P("sec", "elem"),
        ),
        out_specs=P("sec", None, "elem"),
        check_vma=False,
    )
```
